128 devices in a mesh: ctx: 32 (over z_hi, x, y), tp: 4 (over z_lo, core).
Axes of the slice: x: 4, y: 4, z: 4 (z_hi: 2, z_lo: 2; z = z_hi * 2 + z_lo), core: 2. Of those that a mesh axis runs over, the one named last changes fastest.
Arguments:
- tokens: bfloat16 [8192, 4096], P('ctx', 'tp'), may hold values from -6 to 6
- proj_weight: bfloat16 [3, 4096, 4096], P(None, None, 'tp'), may hold values from -0.09375 to 0.09375
- short_taps: float32 [3, 3, 4096], P(None, None, 'tp'), may hold values from -3 to 3
- residues: float32 [4096, 16], P('tp'), may hold values from -0.12 to 0.12
- rates: float32 [4096, 16], P('tp'), may hold values from 3.6621095e-05 to 0.05
- skip: float32 [4096], P('tp'), may hold values from -4 to 4
Outputs:
- gated: bfloat16 [8192, 4096], P('ctx', 'tp')
The draws below stay inside these ranges and needn't reach their ends.
All inputs are finite; a program needn't handle non-finite values.
Results may differ from the reference program's by a relative error of at most 0.0085.
Values may be sent and summed in bfloat16 or wider, within the bound.
A program may use at most 128 MiB of HBM per device.

```python
import math
import jax
import jax.numpy as jnp
from jax import lax

D = 4096
ORDER = 16
TAPS = 3
SUB = 32
TOKENS = 8192


def shard_levels(own_key, shape, pieces, low, high):
    gain, own = 1.0, jax.random.fold_in(own_key, 6)
    for position, blocks in pieces:
        steps = jnp.exp(jax.random.uniform(jax.random.fold_in(own, position), (blocks,), jnp.float32, low / len(pieces), high / len(pieces)))
        gain = gain * jnp.repeat(steps, shape[position] // blocks).reshape([-1 if axis == position else 1 for axis in range(len(shape))])
    return gain


def noise(own_key, shape, deviation, most, shards=(), dtype=jnp.bfloat16):
    values = deviation * jax.random.normal(own_key, shape, jnp.float32)
    if shards:
        values = values * shard_levels(own_key, shape, shards, -0.22, 0.18)
    return jnp.clip(values, -most, most).astype(dtype)


def setup_inputs(seed: int = 0) -> dict:
    key_list = jax.random.split(jax.random.key(seed), 7)
    tokens = noise(key_list[0], (TOKENS, D), 1.0, 6.0, ((0, 32), (1, 4)))
    proj_weight = noise(key_list[1], (3, D, D), D ** -0.5, 0.09375, ((2, 4),))
    short_taps = noise(key_list[2], (3, TAPS, D), 0.6, 3.0, ((2, 4),), jnp.float32)
    residues = noise(key_list[3], (D, ORDER), 0.02, 0.12, ((0, 4),), jnp.float32)
    rates = jnp.clip(jnp.exp(math.log(0.05) - 7.219154 * jax.random.uniform(key_list[4], (D, ORDER), jnp.float32) ** shard_levels(key_list[4], (D, ORDER), ((0, 4),), -0.2, 0.2)), 3.662109520519152e-05, 0.05)
    skip = noise(key_list[5], (D,), 1.0, 4.0, ((0, 4),), jnp.float32)
    return dict(tokens=tokens, proj_weight=proj_weight, short_taps=short_taps, residues=residues, rates=rates, skip=skip)


def long_conv(source_f, residues, rates, sub, init):
    length, width = source_f.shape
    res_t = residues.T
    rate_t = rates.T
    lags = jnp.arange(sub).astype(jnp.float32)
    filt = jnp.sum(res_t[None] * jnp.exp(-rate_t[None] * lags[:, None, None]), axis=1)
    rows = jnp.arange(sub)
    lag = rows[:, None] - rows[None, :]
    band = jnp.where((lag >= 0)[:, :, None], filt[jnp.clip(lag, 0, sub - 1)], 0.0)
    back = jnp.exp(-rate_t[None] * (sub - 1.0 - lags)[:, None, None])
    ahead = res_t[None] * jnp.exp(-rate_t[None] * (lags + 1.0)[:, None, None])
    factor = jnp.exp(-rate_t * float(sub))

    def step(state, src):
        out = jnp.sum(band * src[None], axis=1) + jnp.sum(ahead * state[None], axis=1)
        state = factor * state + jnp.sum(back * src[:, None, :], axis=0)
        return state, out

    final, outs = lax.scan(step, init, source_f.reshape(length // sub, sub, width))
    return final, outs.reshape(length, width)


def reference(tokens, proj_weight, short_taps, residues, rates, skip):
    taps = short_taps.shape[1]
    projected = jnp.stack([jnp.dot(tokens, proj_weight[j], preferred_element_type=jnp.float32) for j in range(3)]).astype(jnp.bfloat16)
    padded = jnp.pad(projected.astype(jnp.float32), ((0, 0), (taps - 1, 0), (0, 0)))
    mixed = sum(short_taps[:, m][:, None, :] * padded[:, taps - 1 - m: taps - 1 - m + TOKENS] for m in range(taps))
    source = (mixed[1] * mixed[2]).astype(jnp.bfloat16)
    init = jnp.zeros((ORDER, D), jnp.float32)
    _, conv = long_conv(source.astype(jnp.float32), residues, rates, SUB, init)
    return (mixed[0] * (conv + skip[None, :] * source.astype(jnp.float32))).astype(jnp.bfloat16)
```

```python
import jax
import jax.numpy as jnp
from jax import lax
from jax.experimental import pallas as pl
from jax.experimental.pallas import tpu as pltpu
from jax.sharding import PartitionSpec as P

MESH = pl.DeviceIdType.MESH
F32, BF16 = jnp.float32, jnp.bfloat16

ROWS = 256
HALO = 16
M = HALO + ROWS
WIDTH = 1024
ORDER = 16
LANE, SUBL = 128, 8
TILE = 256
TILES = WIDTH // TILE
NY = 4
STEP = 16
CHUNKS = ((0, 256), (256, 256), (512, 256), (768, 128), (896, 128))


def kernel(
    tokens, weight, taps, residues, rates, skip, out,
    w, x, acc, proj, src, base, gate, power, fac, fac_step, res, tail, pack, rim_out, rim_in, rim,
    taps_v, taps_t, rates_v, res_v, skip_v, state, row_in, row_tot, grid_in, wpre, wtot,
    w_sem, tok_sem, par_sem, sib_s, sib_r, far_s, far_r, fwd_s, fwd_r,
    rim_s, rim_r, row_s, row_r, grid_s, grid_r,
):
    ctx, tp = lax.axis_index("ctx"), lax.axis_index("tp")
    n_ctx = lax.axis_size("ctx")
    n_rows = n_ctx // NY
    y, g = ctx % NY, ctx // NY

    def partner(s):
        return (tp + 1 - 2 * (tp % 2), (tp + 2) % 4, 3 - tp)[s - 1] if s else tp

    def w_copy(s, j):
        rows = pl.ds(pl.multiple_of(partner(s) * WIDTH, WIDTH), WIDTH)
        return pltpu.make_async_copy(weight.at[j, rows, :], w.at[s, j], w_sem.at[s, j])

    own_copy = pltpu.make_async_copy(tokens, x.at[0, pl.ds(HALO, ROWS), :], tok_sem.at[0])
    tail_copy = pltpu.make_async_copy(tokens.at[pl.ds(ROWS - 16, 16), :], rim, tok_sem.at[1])
    par_copies = [
        pltpu.make_async_copy(a, b, par_sem.at[i])
        for i, (a, b) in enumerate(
            ((taps, taps_v), (residues, res_v), (rates, rates_v), (skip, skip_v))
        )
    ]
    tail_copy.start()
    own_copy.start()
    for s in range(4):
        for j in range(3):
            w_copy(s, j).start()
        if s == 0:
            for c in par_copies:
                c.start()

    barrier = pltpu.get_barrier_semaphore()

    def greet(c, t):
        pl.semaphore_signal(barrier, inc=1, device_id={"ctx": c, "tp": t}, device_id_type=MESH)

    greet(ctx, partner(1))
    greet(ctx, partner(2))
    for d in range(1, NY):
        greet(ctx - y + (y + NY - d) % NY, tp)

    @pl.when(ctx > 0)
    def _():
        for s in range(4):
            greet(ctx - 1, partner(s))

    @pl.loop(0, g)
    def _(k):
        greet(k * NY + y, tp)

    heard = 2 + (NY - 1) + 4 * jnp.where(ctx < n_ctx - 1, 1, 0) + (n_rows - 1 - g)
    pl.semaphore_wait(barrier, heard)

    def sib_copy():
        return pltpu.make_async_remote_copy(
            tokens, x.at[1, pl.ds(HALO, ROWS), :], sib_s, sib_r,
            device_id={"ctx": ctx, "tp": partner(1)}, device_id_type=MESH)

    def far_copy(i):
        cols = pl.ds(*CHUNKS[i])
        return pltpu.make_async_remote_copy(
            tokens.at[:, cols], x.at[2, pl.ds(HALO, ROWS), cols], far_s.at[i], far_r.at[i],
            device_id={"ctx": ctx, "tp": partner(2)}, device_id_type=MESH)

    def fwd_copy(i):
        cols = pl.ds(*CHUNKS[i])
        return pltpu.make_async_remote_copy(
            x.at[2, pl.ds(HALO, ROWS), cols], x.at[3, pl.ds(HALO, ROWS), cols],
            fwd_s.at[i], fwd_r.at[i],
            device_id={"ctx": ctx, "tp": partner(1)}, device_id_type=MESH)

    def rim_copy(s):
        return pltpu.make_async_remote_copy(
            rim_out, rim_in.at[s], rim_s.at[s], rim_r.at[s],
            device_id={"ctx": ctx + 1, "tp": partner(s)}, device_id_type=MESH)

    for i in range(len(CHUNKS)):
        far_copy(i).start()
    sib_copy().start()

    tail_copy.wait()
    tail[...] = rim[...].astype(F32)
    for c in range(SUBL):
        pack[2 * c:2 * c + 2, :] = tail[14:16, c * LANE:(c + 1) * LANE]
    rim_out[...] = pack[...].astype(BF16)

    @pl.when(ctx < n_ctx - 1)
    def _():
        for s in range(4):
            rim_copy(s).start()

    for c in par_copies:
        c.wait()

    def by_position(ref, first, value):
        count = value.shape[0]
        for c in range(SUBL):
            ref[pl.ds(first + c, count, stride=SUBL), :] = value[:, c * LANE:(c + 1) * LANE]

    for j in range(3):
        by_position(taps_t, j * 3 * SUBL, taps_v[j])
    by_position(res, 0, res_v[...])
    by_position(fac, 0, rates_v[...])
    rate = fac[...]
    for d in range(NY):
        below = (y + NY - d) % NY
        wtot[d] = jnp.exp(-rate * (ROWS * (NY - 1 - below)).astype(F32))
        if d:
            wpre[d - 1] = jnp.exp(-rate * float(ROWS * (d - 1))) * jnp.where(d <= y, 1.0, 0.0)
    fac_step[0] = jnp.exp(-rate * float(ROWS * NY))
    fac_step[1] = jnp.exp(-rate * (ROWS * y).astype(F32))
    fac[...] = jnp.exp(-rate)

    @pl.loop(0, STEP)
    def _(b):
        power[b] = jnp.exp(-rate * (b + 1).astype(F32))

    tail[...] = jnp.zeros_like(tail)
    for s in range(4):
        @pl.when(ctx > 0)
        def _(s=s):
            rim_copy(s).wait_recv()
            pack[...] = rim_in[s].astype(F32)
            for c in range(SUBL):
                tail[14:16, c * LANE:(c + 1) * LANE] = pack[2 * c:2 * c + 2, :]

        x[s, 0:HALO, :] = tail[...].astype(BF16)

    def tile_of(q):
        return q // TILES, pl.ds(pl.multiple_of((q % TILES) * TILE, TILE), TILE)

    own_copy.wait()
    for j in range(3):
        w_copy(0, j).wait()

        @pl.loop(j * TILES, (j + 1) * TILES)
        def _(q):
            _, cols = tile_of(q)
            acc[q] = jnp.dot(x[0], w[0, j, :, cols], preferred_element_type=F32)

    sib_copy().wait_recv()
    for j in range(3):
        w_copy(1, j).wait()

        @pl.loop(j * TILES, (j + 1) * TILES)
        def _(q):
            _, cols = tile_of(q)
            acc[q] += jnp.dot(x[1], w[1, j, :, cols], preferred_element_type=F32)

    def far_dots(i, q):
        j, cols = tile_of(q)
        first, size = CHUNKS[i]
        k = slice(first, first + size)
        return (
            jnp.dot(x[2, :, k], w[2, j, k, cols], preferred_element_type=F32)
            + jnp.dot(x[3, :, k], w[3, j, k, cols], preferred_element_type=F32)
        )

    last = len(CHUNKS) - 1
    for i in range(last + 1):
        far_copy(i).wait_recv()
        fwd_copy(i).start()
        if i == 0:
            for s in (2, 3):
                for j in range(3):
                    w_copy(s, j).wait()
        if i:
            fwd_copy(i - 1).wait_recv()

            @pl.loop(0, 3 * TILES)
            def _(q, i=i):
                acc[q] += far_dots(i - 1, q)

    def finish(q):
        value = (acc[q] + far_dots(last, q)).astype(BF16).astype(F32)
        first = (q // TILES) * (M * SUBL) + (q % TILES) * (TILE // LANE)
        for c in range(TILE // LANE):
            proj[pl.ds(first + c, M, stride=SUBL), :] = value[:, c * LANE:(c + 1) * LANE]

    fwd_copy(last).wait_recv()

    @pl.loop(TILES, 3 * TILES)
    def _(q):
        finish(q)

    def row(j, t):
        first = (j * M + HALO + t) * SUBL
        return proj[pl.ds(pl.multiple_of(first, SUBL), SUBL), :]

    def at(t):
        return pl.ds(pl.multiple_of(t * SUBL, SUBL), SUBL)

    def tap(j, m):
        first = (j * 3 + m) * SUBL
        return taps_t[first:first + SUBL, :]

    shape = (ORDER, SUBL, LANE)

    def state_step(i, carry):
        s, k1, k2, v1, v2 = carry
        f = fac[...].reshape(shape)
        for u in range(8):
            t = i * 8 + u
            k0, v0 = row(1, t), row(2, t)
            key = tap(1, 0) * k0 + tap(1, 1) * k1 + tap(1, 2) * k2
            value = tap(2, 0) * v0 + tap(2, 1) * v1 + tap(2, 2) * v2
            own = (key * value).astype(BF16).astype(F32)
            src[at(t), :] = own
            s = f * s + own[None]
            k1, k2, v1, v2 = k0, k1, v0, v1
        return s, k1, k2, v1, v2

    zero = jnp.zeros(shape, F32)
    own_state = lax.fori_loop(
        0, ROWS // 8, state_step, (zero, row(1, -1), row(1, -2), row(2, -1), row(2, -2)))[0]
    flat = own_state.reshape(ORDER * SUBL, LANE)
    state[...] = flat.astype(BF16)
    row_tot[0] = flat * wtot[0]

    def row_copy(d):
        return pltpu.make_async_remote_copy(
            state, row_in.at[d - 1], row_s.at[d - 1], row_r.at[d - 1],
            device_id={"ctx": ctx - y + (y + d) % NY, "tp": tp}, device_id_type=MESH)

    for d in range(1, NY):
        row_copy(d).start()

    @pl.loop(0, TILES)
    def _(q):
        finish(q)

    def local_step(i, carry):
        s, g1, g2 = carry
        f, r = fac[...].reshape(shape), res[...].reshape(shape)
        for u in range(8):
            t = i * 8 + u
            own, g0 = src[at(t), :], row(0, t)
            s = f * s + own[None]
            base[at(t), :] = jnp.sum(r * s, axis=0) + skip_v[...] * own
            gate[at(t), :] = tap(0, 0) * g0 + tap(0, 1) * g1 + tap(0, 2) * g2
            g1, g2 = g0, g1
        return s, g1, g2

    half = ROWS // 16
    carry = lax.fori_loop(0, half, local_step, (zero, row(0, -1), row(0, -2)))

    prior, total = jnp.zeros((ORDER * SUBL, LANE), F32), row_tot[0]
    for d in range(1, NY):
        row_copy(d).wait_recv()
        got = row_in[d - 1].astype(F32)
        prior += wpre[d - 1] * got
        total += wtot[d] * got
    row_tot[0] = prior
    for d in range(1, NY):
        row_copy(d).wait_send()
    state[...] = total.astype(BF16)

    def grid_copy(d):
        return pltpu.make_async_remote_copy(
            state, grid_in.at[d - 1], grid_s.at[d - 1], grid_r.at[d - 1],
            device_id={"ctx": ctx + NY * d, "tp": tp}, device_id_type=MESH)

    @pl.loop(1, n_rows - g)
    def _(d):
        grid_copy(d).start()

    lax.fori_loop(half, 2 * half, local_step, carry)

    def add_row(k, total):
        d = g - k
        grid_copy(d).wait_recv()
        return fac_step[0] * total + grid_in[d - 1].astype(F32)

    ahead = lax.fori_loop(0, g, add_row, jnp.zeros((ORDER * SUBL, LANE), F32))
    ahead = row_tot[0] + fac_step[1] * ahead

    def last_step(a, u):
        for b in range(STEP):
            t = a * STEP + b
            conv = jnp.sum(u * power[b].reshape(shape), axis=0) + base[at(t), :]
            base[at(t), :] = gate[at(t), :] * conv
        return u * power[STEP - 1].reshape(shape)

    lax.fori_loop(0, ROWS // STEP, last_step, (res[...] * ahead).reshape(shape))
    for c in range(SUBL):
        out[:, c * LANE:(c + 1) * LANE] = base[pl.ds(c, ROWS, stride=SUBL), :].astype(BF16)

    sib_copy().wait_send()
    for i in range(last + 1):
        far_copy(i).wait_send()
        fwd_copy(i).wait_send()

    @pl.when(ctx < n_ctx - 1)
    def _():
        for s in range(4):
            rim_copy(s).wait_send()

    @pl.loop(1, n_rows - g)
    def _(d):
        grid_copy(d).wait_send()


def shards(tokens, proj_weight, short_taps, residues, rates, skip):
    hbm = pl.BlockSpec(memory_space=pltpu.HBM)
    n_rows = lax.axis_size("ctx") // NY
    chunks = len(CHUNKS)
    flat = (ORDER * SUBL, LANE)
    dma = pltpu.SemaphoreType.DMA
    return pl.pallas_call(
        kernel,
        out_shape=jax.ShapeDtypeStruct((ROWS, WIDTH), BF16),
        in_specs=[hbm] * 6,
        out_specs=pl.BlockSpec(memory_space=pltpu.VMEM),
        scratch_shapes=[
            pltpu.VMEM((4, 3, WIDTH, WIDTH), BF16),
            pltpu.VMEM((4, M, WIDTH), BF16),
            pltpu.VMEM((3 * TILES, M, TILE), F32),
            pltpu.VMEM((3 * M * SUBL, LANE), F32),
            pltpu.VMEM((ROWS * SUBL, LANE), F32),
            pltpu.VMEM((ROWS * SUBL, LANE), F32),
            pltpu.VMEM((ROWS * SUBL, LANE), F32),
            pltpu.VMEM((STEP, *flat), F32),
            pltpu.VMEM(flat, F32),
            pltpu.VMEM((2, *flat), F32),
            pltpu.VMEM(flat, F32),
            pltpu.VMEM((16, WIDTH), F32),
            pltpu.VMEM((16, LANE), F32),
            pltpu.VMEM((16, LANE), BF16),
            pltpu.VMEM((4, 16, LANE), BF16),
            pltpu.VMEM((16, WIDTH), BF16),
            pltpu.VMEM((3, 3, WIDTH), F32),
            pltpu.VMEM((9 * SUBL, LANE), F32),
            pltpu.VMEM((ORDER, WIDTH), F32),
            pltpu.VMEM((ORDER, WIDTH), F32),
            pltpu.VMEM((SUBL, LANE), F32),
            pltpu.VMEM(flat, BF16),
            pltpu.VMEM((NY - 1, *flat), BF16),
            pltpu.VMEM((1, *flat), F32),
            pltpu.VMEM((n_rows - 1, *flat), BF16),
            pltpu.VMEM((NY - 1, *flat), F32),
            pltpu.VMEM((NY, *flat), F32),
            dma((4, 3)),
            dma((2,)),
            dma((4,)),
            dma, dma,
            dma((chunks,)), dma((chunks,)),
            dma((chunks,)), dma((chunks,)),
            dma((4,)), dma((4,)),
            dma((NY - 1,)), dma((NY - 1,)),
            dma((n_rows - 1,)), dma((n_rows - 1,)),
        ],
        compiler_params=pltpu.CompilerParams(
            collective_id=0, has_side_effects=True, vmem_limit_bytes=56 * 2**20),
        name="hyena",
    )(tokens, proj_weight, short_taps, residues.T, rates.T, skip.reshape(SUBL, LANE))


def solution(mesh):
    return jax.shard_map(
        shards,
        mesh=mesh,
        in_specs=(
            P("ctx", "tp"),
            P(None, None, "tp"),
            P(None, None, "tp"),
            P("tp", None),
            P("tp", None),
            P("tp"),
        ),
        out_specs=P("ctx", "tp"),
        check_vma=False,
    )
```

```python
import jax
import jax.numpy as jnp
from jax import lax
from jax.experimental import pallas as pl
from jax.experimental.pallas import tpu as pltpu
from jax.sharding import PartitionSpec as P

MESH = pl.DeviceIdType.MESH
F32, BF16 = jnp.float32, jnp.bfloat16

ROWS = 256
HALO = 16
M = HALO + ROWS
WIDTH = 1024
ORDER = 16
LANE, SUBL = 128, 8
TILE = 256
TILES = WIDTH // TILE
NY = 4
STEP = 16
CHUNKS = ((0, 256), (256, 256), (512, 256), (768, 128), (896, 128))


def kernel(
    tokens, weight, taps, residues, rates, skip, out,
    w, x, acc, proj, src, base, gate, power, fac, fac_step, res, tail, pack, rim_out, rim_in, rim,
    taps_v, taps_t, rates_v, res_v, skip_v, state, row_sum, row_in, row_tot, grid_in, wpre, wtot,
    w_sem, tok_sem, par_sem, sib_s, sib_r, far_s, far_r, fwd_s, fwd_r,
    rim_s, rim_r, row_s, row_r, grid_s, grid_r, rim_ok, row_ok, grid_ok,
):
    ctx, tp = lax.axis_index("ctx"), lax.axis_index("tp")
    n_ctx = lax.axis_size("ctx")
    n_rows = n_ctx // NY
    y, g = ctx % NY, ctx // NY

    def partner(s):
        return (tp + 1 - 2 * (tp % 2), (tp + 2) % 4, 3 - tp)[s - 1] if s else tp

    def w_copy(s, j):
        rows = pl.ds(pl.multiple_of(partner(s) * WIDTH, WIDTH), WIDTH)
        return pltpu.make_async_copy(weight.at[j, rows, :], w.at[s, j], w_sem.at[s, j])

    own_copy = pltpu.make_async_copy(tokens, x.at[0, pl.ds(HALO, ROWS), :], tok_sem.at[0])
    tail_copy = pltpu.make_async_copy(tokens.at[pl.ds(ROWS - 16, 16), :], rim, tok_sem.at[1])
    par_copies = [
        pltpu.make_async_copy(a, b, par_sem.at[i])
        for i, (a, b) in enumerate(
            ((taps, taps_v), (residues, res_v), (rates, rates_v), (skip, skip_v))
        )
    ]
    tail_copy.start()
    own_copy.start()
    for s in range(4):
        for j in range(3):
            w_copy(s, j).start()
        if s == 0:
            for c in par_copies:
                c.start()

    barrier = pltpu.get_barrier_semaphore()

    def greet(c, t):
        pl.semaphore_signal(barrier, inc=1, device_id={"ctx": c, "tp": t}, device_id_type=MESH)

    greet(ctx, partner(1))
    greet(ctx, partner(2))

    @pl.when(ctx < n_ctx - 1)
    def _():
        for s in range(4):
            greet(ctx + 1, partner(s))

    @pl.loop(y + 1, NY)
    def _(k):
        greet(g * NY + k, tp)

    @pl.loop(g + 1, n_rows)
    def _(k):
        greet(k * NY + y, tp)

    pl.semaphore_wait(barrier, 2 + 4 * jnp.where(ctx > 0, 1, 0) + y + g)

    def sib_copy():
        return pltpu.make_async_remote_copy(
            tokens, x.at[1, pl.ds(HALO, ROWS), :], sib_s, sib_r,
            device_id={"ctx": ctx, "tp": partner(1)}, device_id_type=MESH)

    def far_copy(i):
        cols = pl.ds(*CHUNKS[i])
        return pltpu.make_async_remote_copy(
            tokens.at[:, cols], x.at[2, pl.ds(HALO, ROWS), cols], far_s.at[i], far_r.at[i],
            device_id={"ctx": ctx, "tp": partner(2)}, device_id_type=MESH)

    def fwd_copy(i):
        cols = pl.ds(*CHUNKS[i])
        return pltpu.make_async_remote_copy(
            x.at[2, pl.ds(HALO, ROWS), cols], x.at[3, pl.ds(HALO, ROWS), cols],
            fwd_s.at[i], fwd_r.at[i],
            device_id={"ctx": ctx, "tp": partner(1)}, device_id_type=MESH)

    def rim_copy(s):
        return pltpu.make_async_remote_copy(
            rim_out, rim_in.at[s], rim_s.at[s], rim_r.at[s],
            device_id={"ctx": ctx + 1, "tp": partner(s)}, device_id_type=MESH)

    for i in range(len(CHUNKS)):
        far_copy(i).start()
    sib_copy().start()

    def answer(sem, c, t=tp):
        pl.semaphore_signal(sem, inc=1, device_id={"ctx": c, "tp": t}, device_id_type=MESH)

    @pl.when(ctx > 0)
    def _():
        for s in range(4):
            answer(rim_ok, ctx - 1, partner(s))

    @pl.loop(0, y)
    def _(k):
        answer(row_ok, g * NY + k)

    @pl.loop(0, g)
    def _(k):
        answer(grid_ok, k * NY + y)

    tail_copy.wait()
    tail[...] = rim[...].astype(F32)
    for c in range(SUBL):
        pack[2 * c:2 * c + 2, :] = tail[14:16, c * LANE:(c + 1) * LANE]
    rim_out[...] = pack[...].astype(BF16)

    for c in par_copies:
        c.wait()

    def by_position(ref, first, value):
        count = value.shape[0]
        for c in range(SUBL):
            ref[pl.ds(first + c, count, stride=SUBL), :] = value[:, c * LANE:(c + 1) * LANE]

    for j in range(3):
        by_position(taps_t, j * 3 * SUBL, taps_v[j])
    by_position(res, 0, res_v[...])
    by_position(fac, 0, rates_v[...])
    rate = fac[...]
    for d in range(NY):
        below = (y + NY - d) % NY
        wtot[d] = jnp.exp(-rate * (ROWS * (NY - 1 - below)).astype(F32))
        if d:
            wpre[d - 1] = jnp.exp(-rate * float(ROWS * (d - 1))) * jnp.where(d <= y, 1.0, 0.0)
    fac_step[0] = jnp.exp(-rate * float(ROWS * NY))
    fac_step[1] = jnp.exp(-rate * (ROWS * y).astype(F32))
    fac[...] = jnp.exp(-rate)

    @pl.loop(0, STEP)
    def _(b):
        power[b] = jnp.exp(-rate * (b + 1).astype(F32))

    def tile_of(q):
        return q // TILES, slice((q % TILES) * TILE, (q % TILES + 1) * TILE)

    own_copy.wait()
    for j in range(3):
        w_copy(0, j).wait()

        for q in range(j * TILES, (j + 1) * TILES):
            _, cols = tile_of(q)
            acc[q, HALO:] = jnp.dot(x[0, HALO:], w[0, j, :, cols], preferred_element_type=F32)

    @pl.when(ctx < n_ctx - 1)
    def _():
        pl.semaphore_wait(rim_ok, 4)
        for s in range(4):
            rim_copy(s).start()

    sib_copy().wait_recv()
    for j in range(3):
        w_copy(1, j).wait()

        for q in range(j * TILES, (j + 1) * TILES):
            _, cols = tile_of(q)
            acc[q, HALO:] += jnp.dot(x[1, HALO:], w[1, j, :, cols], preferred_element_type=F32)

    def far_dots(i, q):
        j, cols = tile_of(q)
        first, size = CHUNKS[i]
        k = slice(first, first + size)
        left = jnp.concatenate([x[2, :, k], x[3, :, k]], axis=1)
        right = jnp.concatenate([w[2, j, k, cols], w[3, j, k, cols]], axis=0)
        return jnp.dot(left, right, preferred_element_type=F32)

    last = len(CHUNKS) - 1
    for i in range(last + 1):
        far_copy(i).wait_recv()
        fwd_copy(i).start()
        if i == 0:
            tail[...] = jnp.zeros_like(tail)
            for s in range(4):
                @pl.when(ctx > 0)
                def _(s=s):
                    rim_copy(s).wait_recv()
                    pack[...] = rim_in[s].astype(F32)
                    for c in range(SUBL):
                        tail[14:16, c * LANE:(c + 1) * LANE] = pack[2 * c:2 * c + 2, :]

                x[s, 0:HALO, :] = tail[...].astype(BF16)

            for q in range(3 * TILES):
                j, cols = tile_of(q)
                acc[q, 0:HALO] = (
                    jnp.dot(x[0, 0:HALO], w[0, j, :, cols], preferred_element_type=F32)
                    + jnp.dot(x[1, 0:HALO], w[1, j, :, cols], preferred_element_type=F32)
                )
            for s in (2, 3):
                for j in range(3):
                    w_copy(s, j).wait()
        if i:
            fwd_copy(i - 1).wait_recv()

            for q in range(3 * TILES):
                acc[q] += far_dots(i - 1, q)

    def finish(q):
        value = (acc[q] + far_dots(last, q)).astype(BF16).astype(F32)
        first = (q // TILES) * (M * SUBL) + (q % TILES) * (TILE // LANE)
        for c in range(TILE // LANE):
            proj[pl.ds(first + c, M, stride=SUBL), :] = value[:, c * LANE:(c + 1) * LANE]

    fwd_copy(last).wait_recv()

    for q in range(TILES, 3 * TILES):
        finish(q)

    def row(j, t):
        first = (j * M + HALO + t) * SUBL
        return proj[pl.ds(pl.multiple_of(first, SUBL), SUBL), :]

    def at(t):
        return pl.ds(pl.multiple_of(t * SUBL, SUBL), SUBL)

    def tap(j, m):
        first = (j * 3 + m) * SUBL
        return taps_t[first:first + SUBL, :]

    shape = (ORDER, SUBL, LANE)

    def state_step(i, carry):
        s, k1, k2, v1, v2 = carry
        f = fac[...].reshape(shape)
        for u in range(8):
            t = i * 8 + u
            k0, v0 = row(1, t), row(2, t)
            key = tap(1, 0) * k0 + tap(1, 1) * k1 + tap(1, 2) * k2
            value = tap(2, 0) * v0 + tap(2, 1) * v1 + tap(2, 2) * v2
            own = (key * value).astype(BF16).astype(F32)
            src[at(t), :] = own
            s = f * s + own[None]
            k1, k2, v1, v2 = k0, k1, v0, v1
        return s, k1, k2, v1, v2

    zero = jnp.zeros(shape, F32)
    own_state = lax.fori_loop(
        0, ROWS // 8, state_step, (zero, row(1, -1), row(1, -2), row(2, -1), row(2, -2)))[0]
    flat = own_state.reshape(ORDER * SUBL, LANE)
    state[...] = flat.astype(BF16)
    row_tot[0] = flat * wtot[0]

    def row_copy(d):
        return pltpu.make_async_remote_copy(
            state, row_in.at[d - 1], row_s.at[d - 1], row_r.at[d - 1],
            device_id={"ctx": ctx - y + (y + d) % NY, "tp": tp}, device_id_type=MESH)

    @pl.when(y < NY - 1)
    def _():
        pl.semaphore_wait(row_ok, NY - 1 - y)

    for d in range(1, NY):
        row_copy(d).start()

    for q in range(TILES):
        finish(q)

    def local_step(i, carry):
        s, g1, g2 = carry
        f, r = fac[...].reshape(shape), res[...].reshape(shape)
        for u in range(8):
            t = i * 8 + u
            own, g0 = src[at(t), :], row(0, t)
            s = f * s + own[None]
            base[at(t), :] = jnp.sum(r * s, axis=0) + skip_v[...] * own
            gate[at(t), :] = tap(0, 0) * g0 + tap(0, 1) * g1 + tap(0, 2) * g2
            g1, g2 = g0, g1
        return s, g1, g2

    lax.fori_loop(0, ROWS // 8, local_step, (zero, row(0, -1), row(0, -2)))

    prior, total = jnp.zeros((ORDER * SUBL, LANE), F32), row_tot[0]
    for d in range(1, NY):
        row_copy(d).wait_recv()
        got = row_in[d - 1].astype(F32)
        prior += wpre[d - 1] * got
        total += wtot[d] * got
    row_tot[0] = prior
    row_sum[...] = total.astype(BF16)

    def grid_copy(d):
        return pltpu.make_async_remote_copy(
            row_sum, grid_in.at[d - 1], grid_s.at[d - 1], grid_r.at[d - 1],
            device_id={"ctx": ctx + NY * d, "tp": tp}, device_id_type=MESH)

    @pl.when(g < n_rows - 1)
    def _():
        pl.semaphore_wait(grid_ok, n_rows - 1 - g)

    @pl.loop(1, n_rows - g)
    def _(d):
        grid_copy(d).start()

    def add_row(k, total):
        d = g - k
        grid_copy(d).wait_recv()
        return fac_step[0] * total + grid_in[d - 1].astype(F32)

    ahead = lax.fori_loop(0, g, add_row, jnp.zeros((ORDER * SUBL, LANE), F32))
    ahead = row_tot[0] + fac_step[1] * ahead

    def last_step(a, u):
        for b in range(STEP):
            t = a * STEP + b
            conv = jnp.sum(u * power[b].reshape(shape), axis=0) + base[at(t), :]
            base[at(t), :] = gate[at(t), :] * conv
        return u * power[STEP - 1].reshape(shape)

    lax.fori_loop(0, ROWS // STEP, last_step, (res[...] * ahead).reshape(shape))
    for c in range(SUBL):
        out[:, c * LANE:(c + 1) * LANE] = base[pl.ds(c, ROWS, stride=SUBL), :].astype(BF16)

    for d in range(1, NY):
        row_copy(d).wait_send()
    sib_copy().wait_send()
    for i in range(last + 1):
        far_copy(i).wait_send()
        fwd_copy(i).wait_send()

    @pl.when(ctx < n_ctx - 1)
    def _():
        for s in range(4):
            rim_copy(s).wait_send()

    @pl.loop(1, n_rows - g)
    def _(d):
        grid_copy(d).wait_send()


def shards(tokens, proj_weight, short_taps, residues, rates, skip):
    hbm = pl.BlockSpec(memory_space=pltpu.HBM)
    n_rows = lax.axis_size("ctx") // NY
    chunks = len(CHUNKS)
    flat = (ORDER * SUBL, LANE)
    dma = pltpu.SemaphoreType.DMA
    return pl.pallas_call(
        kernel,
        out_shape=pltpu.VMEM((ROWS, WIDTH), BF16),
        in_specs=[hbm] * 6,
        out_specs=pl.BlockSpec(memory_space=pltpu.VMEM),
        scratch_shapes=[
            pltpu.VMEM((4, 3, WIDTH, WIDTH), BF16),
            pltpu.VMEM((4, M, WIDTH), BF16),
            pltpu.VMEM((3 * TILES, M, TILE), F32),
            pltpu.VMEM((3 * M * SUBL, LANE), F32),
            pltpu.VMEM((ROWS * SUBL, LANE), F32),
            pltpu.VMEM((ROWS * SUBL, LANE), F32),
            pltpu.VMEM((ROWS * SUBL, LANE), F32),
            pltpu.VMEM((STEP, *flat), F32),
            pltpu.VMEM(flat, F32),
            pltpu.VMEM((2, *flat), F32),
            pltpu.VMEM(flat, F32),
            pltpu.VMEM((16, WIDTH), F32),
            pltpu.VMEM((16, LANE), F32),
            pltpu.VMEM((16, LANE), BF16),
            pltpu.VMEM((4, 16, LANE), BF16),
            pltpu.VMEM((16, WIDTH), BF16),
            pltpu.VMEM((3, 3, WIDTH), F32),
            pltpu.VMEM((9 * SUBL, LANE), F32),
            pltpu.VMEM((ORDER, WIDTH), F32),
            pltpu.VMEM((ORDER, WIDTH), F32),
            pltpu.VMEM((SUBL, LANE), F32),
            pltpu.VMEM(flat, BF16),
            pltpu.VMEM(flat, BF16),
            pltpu.VMEM((NY - 1, *flat), BF16),
            pltpu.VMEM((1, *flat), F32),
            pltpu.VMEM((n_rows - 1, *flat), BF16),
            pltpu.VMEM((NY - 1, *flat), F32),
            pltpu.VMEM((NY, *flat), F32),
            dma((4, 3)),
            dma((2,)),
            dma((4,)),
            dma, dma,
            dma((chunks,)), dma((chunks,)),
            dma((chunks,)), dma((chunks,)),
            dma((4,)), dma((4,)),
            dma((NY - 1,)), dma((NY - 1,)),
            dma((n_rows - 1,)), dma((n_rows - 1,)),
            *[pltpu.SemaphoreType.REGULAR] * 3,
        ],
        compiler_params=pltpu.CompilerParams(
            collective_id=0, has_side_effects=True, vmem_limit_bytes=56 * 2**20),
        name="hyena",
    )(tokens, proj_weight, short_taps, residues.T, rates.T, skip.reshape(SUBL, LANE))


def solution(mesh):
    return jax.shard_map(
        shards,
        mesh=mesh,
        in_specs=(
            P("ctx", "tp"),
            P(None, None, "tp"),
            P(None, None, "tp"),
            P("tp", None),
            P("tp", None),
            P("tp"),
        ),
        out_specs=P("ctx", "tp"),
        check_vma=False,
    )
```

```python
import jax
import jax.numpy as jnp
from jax import lax
from jax.experimental import pallas as pl
from jax.experimental.pallas import tpu as pltpu
from jax.sharding import PartitionSpec as P

MESH = pl.DeviceIdType.MESH
F32, BF16 = jnp.float32, jnp.bfloat16

ROWS = 256
HALF = 128
PAD = 8
M = PAD + ROWS + 2
WIDTH = 1024
ORDER = 16
LANE, SUBL = 128, 8
TILE = 256
TILES = WIDTH // TILE
NY = 4
STEP = 16
CHUNKS = (
    (0, 0, 512), (0, 512, 512),
    (HALF, 0, 512), (HALF, 512, 256), (HALF, 768, 128), (HALF, 896, 128),
)
EARLY = 2


def kernel(
    tokens, weight, taps, residues, rates, skip, out,
    w, x, acc, proj, src, base, gate, power, fac, fac_step, fac_inv, res, rim_out, rim_in, lead_out, lead_in,
    taps_v, taps_t, rates_v, res_v, skip_v, state, row_sum, row_in, row_tot, prior_own, grid_in, wpre, wtot,
    w_sem, tok_sem, par_sem, sib_s, sib_r, far_s, far_r, fwd_s, fwd_r,
    rim_s, rim_r, lead_s, lead_r, row_s, row_r, grid_s, grid_r, rim_ok, lead_ok, row_ok, grid_ok,
):
    ctx, tp = lax.axis_index("ctx"), lax.axis_index("tp")
    n_ctx = lax.axis_size("ctx")
    n_rows = n_ctx // NY
    y, g = ctx % NY, ctx // NY

    def partner(s):
        return (tp + 1 - 2 * (tp % 2), (tp + 2) % 4, 3 - tp)[s - 1] if s else tp

    def w_copy(s, j):
        rows = pl.ds(pl.multiple_of(partner(s) * WIDTH, WIDTH), WIDTH)
        return pltpu.make_async_copy(weight.at[j, rows, :], w.at[s, j], w_sem.at[s, j])

    own_copy = pltpu.make_async_copy(tokens, x.at[0], tok_sem)
    par_copies = [
        pltpu.make_async_copy(a, b, par_sem.at[i])
        for i, (a, b) in enumerate(
            ((taps, taps_v), (residues, res_v), (rates, rates_v), (skip, skip_v))
        )
    ]
    own_copy.start()
    for j in range(3):
        w_copy(0, j).start()
    for c in par_copies:
        c.start()
    for j in range(3):
        w_copy(1, j).start()

    barrier = pltpu.get_barrier_semaphore()

    def greet(c, t):
        pl.semaphore_signal(barrier, inc=1, device_id={"ctx": c, "tp": t}, device_id_type=MESH)

    greet(ctx, partner(1))
    greet(ctx, partner(2))

    @pl.when((y == 0) & (ctx > 0))
    def _():
        greet(ctx - 1, tp)

    @pl.loop(y + 1, NY)
    def _(k):
        greet(g * NY + k, tp)

    @pl.loop(g + 1, n_rows)
    def _(k):
        greet(k * NY + y, tp)

    pl.semaphore_wait(barrier, 2 + jnp.where((y == NY - 1) & (ctx < n_ctx - 1), 1, 0) + y + g)

    def sib_copy():
        return pltpu.make_async_remote_copy(
            tokens, x.at[1], sib_s, sib_r,
            device_id={"ctx": ctx, "tp": partner(1)}, device_id_type=MESH)

    def piece(i):
        first, column, columns = CHUNKS[i]
        return pl.ds(first, HALF), pl.ds(column, columns)

    def far_copy(i):
        return pltpu.make_async_remote_copy(
            tokens.at[piece(i)], x.at[2, *piece(i)], far_s.at[i], far_r.at[i],
            device_id={"ctx": ctx, "tp": partner(2)}, device_id_type=MESH)

    def fwd_copy(i):
        return pltpu.make_async_remote_copy(
            x.at[2, *piece(i)], x.at[3, *piece(i)], fwd_s.at[i], fwd_r.at[i],
            device_id={"ctx": ctx, "tp": partner(1)}, device_id_type=MESH)

    def rim_copy():
        return pltpu.make_async_remote_copy(
            rim_out, rim_in, rim_s, rim_r,
            device_id={"ctx": ctx + 1, "tp": tp}, device_id_type=MESH)

    def lead_copy():
        return pltpu.make_async_remote_copy(
            lead_out, lead_in, lead_s, lead_r,
            device_id={"ctx": ctx - 1, "tp": tp}, device_id_type=MESH)

    for i in range(len(CHUNKS)):
        far_copy(i).start()
    sib_copy().start()

    def answer(sem, c):
        pl.semaphore_signal(sem, inc=1, device_id={"ctx": c, "tp": tp}, device_id_type=MESH)

    @pl.when(y > 0)
    def _():
        answer(rim_ok, ctx - 1)

    @pl.when((y == NY - 1) & (ctx < n_ctx - 1))
    def _():
        answer(lead_ok, ctx + 1)

    @pl.loop(0, y)
    def _(k):
        answer(row_ok, g * NY + k)

    @pl.loop(0, g)
    def _(k):
        answer(grid_ok, k * NY + y)

    for c in par_copies:
        c.wait()

    def by_position(ref, first, value):
        count = value.shape[0]
        for c in range(SUBL):
            ref[pl.ds(first + c, count, stride=SUBL), :] = value[:, c * LANE:(c + 1) * LANE]

    for j in range(3):
        by_position(taps_t, j * 3 * SUBL, taps_v[j])
    by_position(res, 0, res_v[...])
    by_position(fac, 0, rates_v[...])
    rate = fac[...]
    for d in range(NY):
        below = (y + NY - d) % NY
        wtot[d] = jnp.exp(-rate * (ROWS * (NY - 1 - below)).astype(F32))
        if d:
            wpre[d - 1] = jnp.exp(-rate * float(ROWS * (d - 1))) * jnp.where(d <= y, 1.0, 0.0)
    fac_step[0] = jnp.exp(-rate * float(ROWS * NY))
    fac_step[1] = jnp.exp(-rate * (ROWS * y).astype(F32))
    fac_inv[...] = jnp.exp(rate)
    fac[...] = jnp.exp(-rate)

    @pl.loop(0, STEP)
    def _(b):
        power[b] = jnp.exp(-rate * (b + 1).astype(F32))

    for j in range(3):
        proj[j * M * SUBL:(j * M + PAD) * SUBL, :] = jnp.zeros((PAD * SUBL, LANE), F32)
        proj[((j + 1) * M - 2) * SUBL:(j + 1) * M * SUBL, :] = jnp.zeros((2 * SUBL, LANE), F32)

    def tile_of(q):
        return q // TILES, slice((q % TILES) * TILE, (q % TILES + 1) * TILE)

    own_copy.wait()
    for j in range(3):
        w_copy(0, j).wait()
        w_copy(2, j).start()
        for q in range(j * TILES, (j + 1) * TILES):
            _, cols = tile_of(q)
            acc[q] = jnp.dot(x[0], w[0, j, :, cols], preferred_element_type=F32)
    sib_copy().wait_recv()
    for j in range(3):
        w_copy(1, j).wait()
        w_copy(3, j).start()
        for q in range(j * TILES, (j + 1) * TILES):
            _, cols = tile_of(q)
            acc[q] += jnp.dot(x[1], w[1, j, :, cols], preferred_element_type=F32)

    def dots(i, q, slots):
        j, cols = tile_of(q)
        first, column, columns = CHUNKS[i]
        r, k = slice(first, first + HALF), slice(column, column + columns)
        left = jnp.concatenate([x[s, r, k] for s in slots], axis=1)
        right = jnp.concatenate([w[s, j, k, cols] for s in slots], axis=0)
        return jnp.dot(left, right, preferred_element_type=F32)

    def add(i, slots):
        r = slice(CHUNKS[i][0], CHUNKS[i][0] + HALF)
        for q in range(3 * TILES):
            acc[q, r] += dots(i, q, slots)

    def finish(i, q, slots):
        first = CHUNKS[i][0]
        value = acc[q, first:first + HALF] + dots(i, q, slots)
        value = value.astype(BF16).astype(F32)
        start = ((q // TILES) * M + PAD + first) * SUBL + (q % TILES) * (TILE // LANE)
        for c in range(TILE // LANE):
            proj[pl.ds(start + c, HALF, stride=SUBL), :] = value[:, c * LANE:(c + 1) * LANE]

    last = len(CHUNKS) - 1
    for i in range(EARLY):
        far_copy(i).wait_recv()
        fwd_copy(i).start()
        if i == 0:
            for j in range(3):
                w_copy(2, j).wait()
        add(i, (2,))
        if i == 0:
            for j in range(3):
                w_copy(3, j).wait()
        fwd_copy(i).wait_recv()
        if i < EARLY - 1:
            add(i, (3,))
    for q in range(3 * TILES):
        finish(EARLY - 1, q, (3,))

    def two_rows(j, t):
        first = (j * M + PAD + t) * SUBL
        return slice(first, first + 2 * SUBL)

    for j in (1, 2):
        lead_out[2 * SUBL * (j - 1):2 * SUBL * j, :] = proj[two_rows(j, 0), :].astype(BF16)

    @pl.when((y == 0) & (ctx > 0))
    def _():
        pl.semaphore_wait(lead_ok, 1)

    @pl.when(ctx > 0)
    def _():
        lead_copy().start()

    def row(j, t):
        first = (j * M + PAD + t) * SUBL
        return proj[pl.ds(pl.multiple_of(first, SUBL), SUBL), :]

    def at(t):
        return pl.ds(pl.multiple_of(t * SUBL, SUBL), SUBL)

    def tap(j, m):
        first = (j * 3 + m) * SUBL
        return taps_t[first:first + SUBL, :]

    shape, flat = (ORDER, SUBL, LANE), (ORDER * SUBL, LANE)

    def mix(j, p0, p1, p2):
        return tap(j, 0) * p0 + tap(j, 1) * p1 + tap(j, 2) * p2

    def source(keys, values):
        return (mix(1, *keys) * mix(2, *values)).astype(BF16).astype(F32)

    def source_at(t):
        return source([row(1, t - d) for d in range(3)], [row(2, t - d) for d in range(3)])

    def state_of(state, start, count, unroll):
        def state_step(i, carry):
            s, k1, k2, v1, v2 = carry
            f = fac[...].reshape(shape)
            for u in range(unroll):
                t = start + i * unroll + u
                k0, v0 = row(1, t), row(2, t)
                own = source((k0, k1, k2), (v0, v1, v2))
                src[at(t), :] = own
                s = f * s + own[None]
                k1, k2, v1, v2 = k0, k1, v0, v1
            return s, k1, k2, v1, v2

        before = [row(j, start - d) for j in (1, 2) for d in (1, 2)]
        return lax.fori_loop(0, count // unroll, state_step, (state, *before))[0]

    first_rows = fac[...].reshape(shape) * source_at(0)[None] + source_at(1)[None]
    first_rows = first_rows * jnp.where(ctx == 0, 1.0, 0.0)
    prior_own[...] = first_rows.reshape(flat)
    row_tot[0] = state_of(first_rows, 2, HALF - 2, 9).reshape(flat)

    for i in range(EARLY, last + 1):
        far_copy(i).wait_recv()
        fwd_copy(i).start()
        if i > EARLY:
            fwd_copy(i - 1).wait_recv()
            add(i - 1, (2, 3))
    fwd_copy(last).wait_recv()
    for q in range(TILES, 3 * TILES):
        finish(last, q, (2, 3))
    own_state = state_of(row_tot[0].reshape(shape), HALF, ROWS - HALF, 8)

    @pl.when(ctx < n_ctx - 1)
    def _():
        lead_copy().wait_recv()
        for j in (1, 2):
            proj[two_rows(j, ROWS), :] = lead_in[2 * SUBL * (j - 1):2 * SUBL * j, :].astype(F32)

    for t in (ROWS, ROWS + 1):
        own_state = fac[...].reshape(shape) * own_state + source_at(t)[None]
    own_state = own_state.reshape(flat)
    state[...] = own_state.astype(BF16)
    row_tot[0] = own_state * wtot[0]

    def row_copy(d):
        return pltpu.make_async_remote_copy(
            state, row_in.at[d - 1], row_s.at[d - 1], row_r.at[d - 1],
            device_id={"ctx": ctx - y + (y + d) % NY, "tp": tp}, device_id_type=MESH)

    @pl.when(y < NY - 1)
    def _():
        pl.semaphore_wait(row_ok, NY - 1 - y)

    for d in range(1, NY):
        row_copy(d).start()

    for q in range(TILES):
        finish(last, q, (2, 3))
    for j in range(3):
        rim_out[2 * SUBL * j:2 * SUBL * (j + 1), :] = proj[two_rows(j, ROWS - 2), :].astype(BF16)

    @pl.when(y < NY - 1)
    def _():
        pl.semaphore_wait(rim_ok, 1)

    @pl.when(ctx < n_ctx - 1)
    def _():
        rim_copy().start()

    def local_rows(first, count, carry):
        s, g1, g2 = carry
        f, r = fac[...].reshape(shape), res[...].reshape(shape)
        for u in range(count):
            t = first + u
            own, g0 = src[at(t), :], row(0, t)
            s = f * s + own[None]
            base[at(t), :] = jnp.sum(r * s, axis=0) + skip_v[...] * own
            gate[at(t), :] = mix(0, g0, g1, g2)
            g1, g2 = g0, g1
        return s, g1, g2

    carry = lax.fori_loop(
        0, (ROWS - 2) // 8, lambda i, carry: local_rows(2 + i * 8, 8, carry),
        (jnp.zeros(shape, F32), row(0, 1), row(0, 0)))
    local_rows(2 + (ROWS - 2) // 8 * 8, (ROWS - 2) % 8, carry)

    prior, total = jnp.zeros(flat, F32), row_tot[0]
    for d in range(1, NY):
        row_copy(d).wait_recv()
        got = row_in[d - 1].astype(F32)
        prior += wpre[d - 1] * got
        total += wtot[d] * got
    row_tot[0] = prior
    row_sum[...] = total.astype(BF16)

    def grid_copy(d):
        return pltpu.make_async_remote_copy(
            row_sum, grid_in.at[d - 1], grid_s.at[d - 1], grid_r.at[d - 1],
            device_id={"ctx": ctx + NY * d, "tp": tp}, device_id_type=MESH)

    @pl.when(g < n_rows - 1)
    def _():
        pl.semaphore_wait(grid_ok, n_rows - 1 - g)

    @pl.loop(1, n_rows - g)
    def _(d):
        grid_copy(d).start()

    @pl.when(ctx > 0)
    def _():
        rim_copy().wait_recv()
        for j in range(3):
            proj[two_rows(j, -2), :] = rim_in[2 * SUBL * j:2 * SUBL * (j + 1), :].astype(F32)

    for t in (0, 1):
        src[at(t), :] = source_at(t)
        base[at(t), :] = skip_v[...] * src[at(t), :]
        gate[at(t), :] = mix(0, *[row(0, t - d) for d in range(3)])

    def add_row(k, total):
        d = g - k
        grid_copy(d).wait_recv()
        return fac_step[0] * total + grid_in[d - 1].astype(F32)

    ahead = lax.fori_loop(0, g, add_row, jnp.zeros(flat, F32))
    ahead = row_tot[0] + fac_step[1] * ahead + prior_own[...]

    def close(t, conv):
        base[at(t), :] = gate[at(t), :] * (conv + base[at(t), :])

    weighted = (res[...] * ahead).reshape(shape)
    close(1, jnp.sum(weighted, axis=0))
    before = (ahead.reshape(shape) - src[at(1), :][None]) * fac_inv[...].reshape(shape)
    close(0, jnp.sum(res[...].reshape(shape) * before, axis=0))

    def last_rows(first, count, u):
        for b in range(count):
            close(first + b, jnp.sum(u * power[b].reshape(shape), axis=0))

    def last_step(a, u):
        last_rows(2 + a * STEP, STEP, u)
        return u * power[STEP - 1].reshape(shape)

    whole = (ROWS - 2) // STEP
    weighted = lax.fori_loop(0, whole, last_step, weighted)
    last_rows(2 + whole * STEP, ROWS - 2 - whole * STEP, weighted)
    for c in range(SUBL):
        out[:, c * LANE:(c + 1) * LANE] = base[pl.ds(c, ROWS, stride=SUBL), :].astype(BF16)

    for d in range(1, NY):
        row_copy(d).wait_send()
    sib_copy().wait_send()
    for i in range(last + 1):
        far_copy(i).wait_send()
        fwd_copy(i).wait_send()

    @pl.when(ctx < n_ctx - 1)
    def _():
        rim_copy().wait_send()

    @pl.when(ctx > 0)
    def _():
        lead_copy().wait_send()

    @pl.loop(1, n_rows - g)
    def _(d):
        grid_copy(d).wait_send()


def shards(tokens, proj_weight, short_taps, residues, rates, skip):
    hbm = pl.BlockSpec(memory_space=pltpu.HBM)
    n_rows = lax.axis_size("ctx") // NY
    chunks = len(CHUNKS)
    flat = (ORDER * SUBL, LANE)
    dma = pltpu.SemaphoreType.DMA
    return pl.pallas_call(
        kernel,
        out_shape=pltpu.VMEM((ROWS, WIDTH), BF16),
        in_specs=[hbm] * 6,
        out_specs=pl.BlockSpec(memory_space=pltpu.VMEM),
        scratch_shapes=[
            pltpu.VMEM((4, 3, WIDTH, WIDTH), BF16),
            pltpu.VMEM((4, ROWS, WIDTH), BF16),
            pltpu.VMEM((3 * TILES, ROWS, TILE), F32),
            pltpu.VMEM((3 * M * SUBL, LANE), F32),
            pltpu.VMEM((ROWS * SUBL, LANE), F32),
            pltpu.VMEM((ROWS * SUBL, LANE), F32),
            pltpu.VMEM((ROWS * SUBL, LANE), F32),
            pltpu.VMEM((STEP, *flat), F32),
            pltpu.VMEM(flat, F32),
            pltpu.VMEM((2, *flat), F32),
            pltpu.VMEM(flat, F32),
            pltpu.VMEM(flat, F32),
            pltpu.VMEM((3 * 2 * SUBL, LANE), BF16),
            pltpu.VMEM((3 * 2 * SUBL, LANE), BF16),
            pltpu.VMEM((2 * 2 * SUBL, LANE), BF16),
            pltpu.VMEM((2 * 2 * SUBL, LANE), BF16),
            pltpu.VMEM((3, 3, WIDTH), F32),
            pltpu.VMEM((9 * SUBL, LANE), F32),
            pltpu.VMEM((ORDER, WIDTH), F32),
            pltpu.VMEM((ORDER, WIDTH), F32),
            pltpu.VMEM((SUBL, LANE), F32),
            pltpu.VMEM(flat, BF16),
            pltpu.VMEM(flat, BF16),
            pltpu.VMEM((NY - 1, *flat), BF16),
            pltpu.VMEM((1, *flat), F32),
            pltpu.VMEM(flat, F32),
            pltpu.VMEM((n_rows - 1, *flat), BF16),
            pltpu.VMEM((NY - 1, *flat), F32),
            pltpu.VMEM((NY, *flat), F32),
            dma((4, 3)),
            dma,
            dma((4,)),
            dma, dma,
            dma((chunks,)), dma((chunks,)),
            dma((chunks,)), dma((chunks,)),
            dma, dma,
            dma, dma,
            dma((NY - 1,)), dma((NY - 1,)),
            dma((n_rows - 1,)), dma((n_rows - 1,)),
            *[pltpu.SemaphoreType.REGULAR] * 4,
        ],
        compiler_params=pltpu.CompilerParams(
            collective_id=0, has_side_effects=True, vmem_limit_bytes=56 * 2**20),
        name="hyena",
    )(tokens, proj_weight, short_taps, residues.T, rates.T, skip.reshape(SUBL, LANE))


def solution(mesh):
    return jax.shard_map(
        shards,
        mesh=mesh,
        in_specs=(
            P("ctx", "tp"),
            P(None, None, "tp"),
            P(None, None, "tp"),
            P("tp", None),
            P("tp", None),
            P("tp"),
        ),
        out_specs=P("ctx", "tp"),
        check_vma=False,
    )
```

```python
import jax
import jax.numpy as jnp
from jax import lax
from jax.experimental import pallas as pl
from jax.experimental.pallas import tpu as pltpu
from jax.sharding import PartitionSpec as P

MESH = pl.DeviceIdType.MESH
F32, BF16 = jnp.float32, jnp.bfloat16

ROWS = 256
HALF = 128
PAD = 8
M = PAD + ROWS
WIDTH = 1024
ORDER = 16
LANE, SUBL = 128, 8
TILE = 256
TILES = WIDTH // TILE
NY = 4
STEP = 16
CHUNKS = (
    (HALF, 0, 512), (HALF, 512, 512),
    (0, 0, 512), (0, 512, 256), (0, 768, 128), (0, 896, 128),
)
LATER = 2


def kernel(
    tokens, weight, taps, residues, rates, skip, out,
    w, x, acc, proj, src, base, gate, done, power, fac, fac_step, fac_part, res, rim_out, rim_in,
    taps_v, taps_t, rates_v, res_v, skip_v, state, row_sum, row_in, row_tot, grid_in, wpre, wtot,
    w_sem, tok_sem, par_sem, sib_s, sib_r, far_s, far_r, fwd_s, fwd_r, cross_s, cross_r,
    rim_s, rim_r, row_s, row_r, grid_s, grid_r, rim_ok, row_ok, grid_ok, seam_ok,
):
    ctx, tp = lax.axis_index("ctx"), lax.axis_index("tp")
    n_ctx = lax.axis_size("ctx")
    n_rows = n_ctx // NY
    y, g = ctx % NY, ctx // NY
    nx = n_rows // 2
    half, xx = g // nx, g % nx
    seam = nx * NY

    def partner(s):
        return (tp + 1 - 2 * (tp % 2), (tp + 2) % 4, 3 - tp)[s - 1] if s else tp

    def w_copy(s, j):
        rows = pl.ds(pl.multiple_of(partner(s) * WIDTH, WIDTH), WIDTH)
        return pltpu.make_async_copy(weight.at[j, rows, :], w.at[s, j], w_sem.at[s, j])

    own_copy = pltpu.make_async_copy(tokens, x.at[0], tok_sem)
    par_copies = [
        pltpu.make_async_copy(a, b, par_sem.at[i])
        for i, (a, b) in enumerate(
            ((taps, taps_v), (residues, res_v), (rates, rates_v), (skip, skip_v))
        )
    ]
    barrier = pltpu.get_barrier_semaphore()

    def greet(c, t):
        pl.semaphore_signal(barrier, inc=1, device_id={"ctx": c, "tp": t}, device_id_type=MESH)

    greet(ctx, partner(1))
    greet(ctx, partner(2))
    greet(ctx, partner(3))

    @pl.when((y == 0) & (xx > 0))
    def _():
        greet(ctx - 1, tp)

    @pl.loop(y + 1, NY)
    def _(k):
        greet(g * NY + k, tp)

    @pl.loop(xx + 1, nx)
    def _(k):
        greet((half * nx + k) * NY + y, tp)

    @pl.when(half == 0)
    def _():
        @pl.loop(xx, nx)
        def _(k):
            greet((nx + k) * NY + y, tp)

    own_copy.start()
    for j in range(3):
        w_copy(0, j).start()
    for c in par_copies:
        c.start()
    for j in range(3):
        w_copy(1, j).start()

    heard = 3 + jnp.where((y == NY - 1) & (xx < nx - 1), 1, 0) + y + xx + half * (xx + 1)
    pl.semaphore_wait(barrier, heard)

    def sib_copy():
        return pltpu.make_async_remote_copy(
            tokens, x.at[1], sib_s, sib_r,
            device_id={"ctx": ctx, "tp": partner(1)}, device_id_type=MESH)

    def piece(i):
        first, column, columns = CHUNKS[i]
        return pl.ds(first, HALF), pl.ds(column, columns)

    def far_copy(i):
        return pltpu.make_async_remote_copy(
            tokens.at[piece(i)], x.at[2, *piece(i)], far_s.at[i], far_r.at[i],
            device_id={"ctx": ctx, "tp": partner(2)}, device_id_type=MESH)

    def fwd_copy(i):
        return pltpu.make_async_remote_copy(
            x.at[2, *piece(i)], x.at[3, *piece(i)], fwd_s.at[i], fwd_r.at[i],
            device_id={"ctx": ctx, "tp": partner(1)}, device_id_type=MESH)

    def cross_copy():
        return pltpu.make_async_remote_copy(
            tokens.at[piece(len(CHUNKS) - 1)], x.at[3, *piece(len(CHUNKS) - 1)], cross_s, cross_r,
            device_id={"ctx": ctx, "tp": partner(3)}, device_id_type=MESH)

    def rim_copy():
        return pltpu.make_async_remote_copy(
            rim_out, rim_in, rim_s, rim_r,
            device_id={"ctx": ctx + 1, "tp": tp}, device_id_type=MESH)

    for i in range(len(CHUNKS)):
        far_copy(i).start()
    cross_copy().start()
    sib_copy().start()

    def answer(sem, c):
        pl.semaphore_signal(sem, inc=1, device_id={"ctx": c, "tp": tp}, device_id_type=MESH)

    @pl.when(y > 0)
    def _():
        answer(rim_ok, ctx - 1)

    @pl.loop(0, y)
    def _(k):
        answer(row_ok, g * NY + k)

    @pl.loop(0, xx)
    def _(k):
        answer(grid_ok, (half * nx + k) * NY + y)

    @pl.when(half == 1)
    def _():
        @pl.loop(0, xx + 1)
        def _(k):
            answer(grid_ok, k * NY + y)

    for c in par_copies:
        c.wait()

    def by_position(ref, first, value):
        count = value.shape[0]
        for c in range(SUBL):
            ref[pl.ds(first + c, count, stride=SUBL), :] = value[:, c * LANE:(c + 1) * LANE]

    for j in range(3):
        by_position(taps_t, j * 3 * SUBL, taps_v[j])
    by_position(res, 0, res_v[...])
    by_position(fac, 0, rates_v[...])
    rate = fac[...]
    for d in range(NY):
        below = (y + NY - d) % NY
        wtot[d] = jnp.exp(-rate * (ROWS * (NY - 1 - below)).astype(F32))
        if d:
            wpre[d - 1] = jnp.exp(-rate * float(ROWS * (d - 1))) * jnp.where(d <= y, 1.0, 0.0)
    fac_step[0] = jnp.exp(-rate * float(ROWS * NY))
    fac_step[1] = jnp.exp(-rate * (ROWS * y).astype(F32))
    fac_part[0] = jnp.exp(-rate * float(ROWS - 2))
    fac_part[1] = jnp.exp(-rate * float(ROWS - HALF - 2))
    fac[...] = jnp.exp(-rate)

    @pl.loop(0, STEP)
    def _(b):
        power[b] = jnp.exp(-rate * (b + 1).astype(F32))

    for j in range(3):
        proj[j * M * SUBL:(j * M + PAD) * SUBL, :] = jnp.zeros((PAD * SUBL, LANE), F32)

    def tile_of(q):
        return q // TILES, slice((q % TILES) * TILE, (q % TILES + 1) * TILE)

    own_copy.wait()
    for j in range(3):
        w_copy(0, j).wait()
        w_copy(2, j).start()
        for q in range(j * TILES, (j + 1) * TILES):
            _, cols = tile_of(q)
            acc[q] = jnp.dot(x[0], w[0, j, :, cols], preferred_element_type=F32)
    @pl.when((half == 1) & (xx < nx - 1))
    def _():
        pl.semaphore_wait(grid_ok, nx - 1 - xx)

        @pl.loop(xx + 1, nx)
        def _(k):
            answer(grid_ok, k * NY + y)

    @pl.when(ctx == seam)
    def _():
        answer(seam_ok, seam - NY)

    sib_copy().wait_recv()
    for j in range(3):
        w_copy(1, j).wait()
        w_copy(3, j).start()
        for q in range(j * TILES, (j + 1) * TILES):
            _, cols = tile_of(q)
            acc[q] += jnp.dot(x[1], w[1, j, :, cols], preferred_element_type=F32)

    @pl.when(y < NY - 1)
    def _():
        pl.semaphore_wait(row_ok, NY - 1 - y)

    @pl.when(ctx == seam - NY)
    def _():
        pl.semaphore_wait(seam_ok, 1)
        answer(rim_ok, seam - 1)

    def dots(i, q, slots):
        j, cols = tile_of(q)
        first, column, columns = CHUNKS[i]
        r, k = slice(first, first + HALF), slice(column, column + columns)
        left = jnp.concatenate([x[s, r, k] for s in slots], axis=1)
        right = jnp.concatenate([w[s, j, k, cols] for s in slots], axis=0)
        return jnp.dot(left, right, preferred_element_type=F32)

    def add(i, slots):
        r = slice(CHUNKS[i][0], CHUNKS[i][0] + HALF)
        for q in range(3 * TILES):
            acc[q, r] += dots(i, q, slots)

    def finish(i, q, slots):
        first = CHUNKS[i][0]
        value = acc[q, first:first + HALF] + dots(i, q, slots)
        value = value.astype(BF16).astype(F32)
        start = ((q // TILES) * M + PAD + first) * SUBL + (q % TILES) * (TILE // LANE)
        for c in range(TILE // LANE):
            proj[pl.ds(start + c, HALF, stride=SUBL), :] = value[:, c * LANE:(c + 1) * LANE]

    last = len(CHUNKS) - 1
    for i in range(LATER):
        far_copy(i).wait_recv()
        fwd_copy(i).start()
        if i == 0:
            for j in range(3):
                w_copy(2, j).wait()
        add(i, (2,))
        if i == 0:
            for j in range(3):
                w_copy(3, j).wait()
        fwd_copy(i).wait_recv()
        if i < LATER - 1:
            add(i, (3,))
    for q in range(3 * TILES):
        finish(LATER - 1, q, (3,))

    for j in range(3):
        first = ((j + 1) * M - 2) * SUBL
        rim_out[2 * SUBL * j:2 * SUBL * (j + 1), :] = proj[first:first + 2 * SUBL, :].astype(BF16)

    @pl.when((y < NY - 1) | (ctx == seam - 1))
    def _():
        pl.semaphore_wait(rim_ok, 1)

    @pl.when(ctx < n_ctx - 1)
    def _():
        rim_copy().start()

    def row(j, t):
        first = (j * M + PAD + t) * SUBL
        return proj[pl.ds(pl.multiple_of(first, SUBL), SUBL), :]

    def at(t):
        return pl.ds(pl.multiple_of(t * SUBL, SUBL), SUBL)

    def tap(j, m):
        first = (j * 3 + m) * SUBL
        return taps_t[first:first + SUBL, :]

    shape, flat = (ORDER, SUBL, LANE), (ORDER * SUBL, LANE)

    def mix(j, p0, p1, p2):
        return tap(j, 0) * p0 + tap(j, 1) * p1 + tap(j, 2) * p2

    def own_source(t, keys, values):
        own = (mix(1, *keys) * mix(2, *values)).astype(BF16).astype(F32)
        src[at(t), :] = own
        return own

    zero = jnp.zeros(shape, F32)

    def state_of(start, count, unroll):
        def state_step(i, carry):
            s, k1, k2, v1, v2 = carry
            f = fac[...].reshape(shape)
            for u in range(unroll):
                t = start + i * unroll + u
                k0, v0 = row(1, t), row(2, t)
                s = f * s + own_source(t, (k0, k1, k2), (v0, v1, v2))[None]
                k1, k2, v1, v2 = k0, k1, v0, v1
            return s, k1, k2, v1, v2

        before = [row(j, start - d) for j in (1, 2) for d in (1, 2)]
        return lax.fori_loop(0, count // unroll, state_step, (zero, *before))[0]

    later_state = state_of(HALF + 2, HALF - 2, 9)
    row_tot[0] = later_state.reshape(flat)

    for i in range(LATER, last + 1):
        far_copy(i).wait_recv()
        if i < last:
            fwd_copy(i).start()
        if i > LATER:
            fwd_copy(i - 1).wait_recv()
            add(i - 1, (2, 3))
    cross_copy().wait_recv()
    for q in range(TILES, 3 * TILES):
        finish(last, q, (2, 3))
    early_state = state_of(2, HALF, 8)

    @pl.when(ctx > 0)
    def _():
        rim_copy().wait_recv()
        for j in range(3):
            first = (j * M + PAD - 2) * SUBL
            proj[first:first + 2 * SUBL, :] = rim_in[2 * SUBL * j:2 * SUBL * (j + 1), :].astype(F32)

    rim_state = fac[...].reshape(shape) * own_source(
        0, [row(1, -d) for d in range(3)], [row(2, -d) for d in range(3)])[None]
    rim_state += own_source(
        1, [row(1, 1 - d) for d in range(3)], [row(2, 1 - d) for d in range(3)])[None]
    own_state = row_tot[0] + fac_part[1] * early_state.reshape(flat)
    own_state += fac_part[0] * rim_state.reshape(flat)
    state[...] = own_state.astype(BF16)

    def row_copy(d):
        return pltpu.make_async_remote_copy(
            state, row_in.at[d - 1], row_s.at[d - 1], row_r.at[d - 1],
            device_id={"ctx": ctx - y + (y + d) % NY, "tp": tp}, device_id_type=MESH)

    for d in (2, 1, 3):
        row_copy(d).start()
    row_tot[0] = own_state * wtot[0]

    for q in range(TILES):
        finish(last, q, (2, 3))

    def local_step(i, carry):
        s, g1, g2 = carry
        f, r = fac[...].reshape(shape), res[...].reshape(shape)
        for u in range(8):
            t = i * 8 + u
            own, g0 = src[at(t), :], row(0, t)
            s = f * s + own[None]
            base[at(t), :] = jnp.sum(r * s, axis=0) + skip_v[...] * own
            gate[at(t), :] = tap(0, 0) * g0 + tap(0, 1) * g1 + tap(0, 2) * g2
            g1, g2 = g0, g1
        return s, g1, g2

    lax.fori_loop(0, ROWS // 8, local_step, (zero, row(0, -1), row(0, -2)))

    total = row_tot[0]
    for d in range(1, NY):
        row_copy(d).wait_recv()
        total += wtot[d] * row_in[d - 1].astype(F32)
    row_sum[...] = total.astype(BF16)

    def grid_copy(d):
        return pltpu.make_async_remote_copy(
            row_sum, grid_in.at[d - 1], grid_s.at[d - 1], grid_r.at[d - 1],
            device_id={"ctx": ctx + NY * d, "tp": tp}, device_id_type=MESH)

    @pl.when(half == 0)
    def _():
        pl.semaphore_wait(grid_ok, n_rows - 1 - g)

    for d in range(1, n_rows):
        @pl.when(d < n_rows - g)
        def _(d=d):
            grid_copy(d).start()

    prior = jnp.zeros(flat, F32)
    for d in range(1, NY):
        prior += wpre[d - 1] * row_in[d - 1].astype(F32)
    row_tot[0] = prior

    for d in range(1, NY):
        row_copy(d).wait_send()
    sib_copy().wait_send()
    for i in range(last + 1):
        far_copy(i).wait_send()
        if i < last:
            fwd_copy(i).wait_send()
    cross_copy().wait_send()

    @pl.when(ctx < n_ctx - 1)
    def _():
        rim_copy().wait_send()

    def add_row(k, total):
        d = g - k
        grid_copy(d).wait_recv()
        return fac_step[0] * total + grid_in[d - 1].astype(F32)

    ahead = lax.fori_loop(0, g, add_row, jnp.zeros(flat, F32))
    ahead = row_tot[0] + fac_step[1] * ahead

    def last_rows(first, u):
        for b in range(STEP):
            t = first + b
            conv = jnp.sum(u * power[b].reshape(shape), axis=0)
            done[at(t), :] = gate[at(t), :] * (conv + base[at(t), :])
        return u * power[STEP - 1].reshape(shape)

    def emit(a):
        rows = pl.ds(pl.multiple_of(a * STEP, STEP), STEP)
        for c in range(SUBL):
            value = done[pl.ds(a * STEP * SUBL + c, STEP, stride=SUBL), :]
            out[rows, c * LANE:(c + 1) * LANE] = value.astype(BF16)

    def last_step(a, u):
        emit(a - 1)
        return last_rows(a * STEP, u)

    weighted = last_rows(0, (res[...] * ahead).reshape(shape))
    lax.fori_loop(1, ROWS // STEP, last_step, weighted)
    emit(ROWS // STEP - 1)

    @pl.loop(1, n_rows - g)
    def _(d):
        grid_copy(d).wait_send()


def shards(tokens, proj_weight, short_taps, residues, rates, skip):
    hbm = pl.BlockSpec(memory_space=pltpu.HBM)
    n_rows = lax.axis_size("ctx") // NY
    chunks = len(CHUNKS)
    flat = (ORDER * SUBL, LANE)
    dma = pltpu.SemaphoreType.DMA
    return pl.pallas_call(
        kernel,
        out_shape=pltpu.VMEM((ROWS, WIDTH), BF16),
        in_specs=[hbm] * 6,
        out_specs=pl.BlockSpec(memory_space=pltpu.VMEM),
        scratch_shapes=[
            pltpu.VMEM((4, 3, WIDTH, WIDTH), BF16),
            pltpu.VMEM((4, ROWS, WIDTH), BF16),
            pltpu.VMEM((3 * TILES, ROWS, TILE), F32),
            pltpu.VMEM((3 * M * SUBL, LANE), F32),
            pltpu.VMEM((ROWS * SUBL, LANE), F32),
            pltpu.VMEM((ROWS * SUBL, LANE), F32),
            pltpu.VMEM((ROWS * SUBL, LANE), F32),
            pltpu.VMEM((ROWS * SUBL, LANE), F32),
            pltpu.VMEM((STEP, *flat), F32),
            pltpu.VMEM(flat, F32),
            pltpu.VMEM((2, *flat), F32),
            pltpu.VMEM((2, *flat), F32),
            pltpu.VMEM(flat, F32),
            pltpu.VMEM((3 * 2 * SUBL, LANE), BF16),
            pltpu.VMEM((3 * 2 * SUBL, LANE), BF16),
            pltpu.VMEM((3, 3, WIDTH), F32),
            pltpu.VMEM((9 * SUBL, LANE), F32),
            pltpu.VMEM((ORDER, WIDTH), F32),
            pltpu.VMEM((ORDER, WIDTH), F32),
            pltpu.VMEM((SUBL, LANE), F32),
            pltpu.VMEM(flat, BF16),
            pltpu.VMEM(flat, BF16),
            pltpu.VMEM((NY - 1, *flat), BF16),
            pltpu.VMEM((1, *flat), F32),
            pltpu.VMEM((n_rows - 1, *flat), BF16),
            pltpu.VMEM((NY - 1, *flat), F32),
            pltpu.VMEM((NY, *flat), F32),
            dma((4, 3)),
            dma,
            dma((4,)),
            dma, dma,
            dma((chunks,)), dma((chunks,)),
            dma((chunks - 1,)), dma((chunks - 1,)),
            dma, dma,
            dma, dma,
            dma((NY - 1,)), dma((NY - 1,)),
            dma((n_rows - 1,)), dma((n_rows - 1,)),
            *[pltpu.SemaphoreType.REGULAR] * 4,
        ],
        compiler_params=pltpu.CompilerParams(
            collective_id=0, has_side_effects=True, vmem_limit_bytes=56 * 2**20),
        name="hyena",
    )(tokens, proj_weight, short_taps, residues.T, rates.T, skip.reshape(SUBL, LANE))


def solution(mesh):
    return jax.shard_map(
        shards,
        mesh=mesh,
        in_specs=(
            P("ctx", "tp"),
            P(None, None, "tp"),
            P(None, None, "tp"),
            P("tp", None),
            P("tp", None),
            P("tp"),
        ),
        out_specs=P("ctx", "tp"),
        check_vma=False,
    )
```

```python
import jax
import jax.numpy as jnp
from jax import lax
from jax.experimental import pallas as pl
from jax.experimental.pallas import tpu as pltpu
from jax.sharding import PartitionSpec as P

MESH = pl.DeviceIdType.MESH
F32, BF16 = jnp.float32, jnp.bfloat16

ROWS = 256
HALF = 128
PAD = 8
M = PAD + ROWS
WIDTH = 1024
ORDER = 16
LANE, SUBL = 128, 8
TILE = 256
TILES = WIDTH // TILE
NY = 4
STEP = 16
CHUNKS = (
    (HALF, 0, 512), (HALF, 512, 512),
    (0, 0, 512), (0, 512, 256), (0, 768, 128), (0, 896, 128),
)
LATER = 2


def kernel(
    tokens, weight, taps, residues, rates, skip, out,
    w, x, acc, proj, src, base, gate, done, fac, fac_step, fac_part, res, rim_out, rim_in,
    taps_v, taps_t, rates_v, res_v, skip_v, state, row_sum, row_in, row_tot, grid_in, wpre, wtot,
    w_sem, tok_sem, par_sem, sib_s, sib_r, far_s, far_r, fwd_s, fwd_r, cross_s, cross_r,
    rim_s, rim_r, row_s, row_r, grid_s, grid_r, rim_ok, row_ok, grid_ok, seam_ok,
):
    ctx, tp = lax.axis_index("ctx"), lax.axis_index("tp")
    n_ctx = lax.axis_size("ctx")
    n_rows = n_ctx // NY
    y, g = ctx % NY, ctx // NY
    nx = n_rows // 2
    half, xx = g // nx, g % nx
    seam = nx * NY

    def partner(s):
        return (tp + 1 - 2 * (tp % 2), (tp + 2) % 4, 3 - tp)[s - 1] if s else tp

    def w_copy(s, j):
        rows = pl.ds(pl.multiple_of(partner(s) * WIDTH, WIDTH), WIDTH)
        return pltpu.make_async_copy(weight.at[j, rows, :], w.at[s, j], w_sem.at[s, j])

    own_copy = pltpu.make_async_copy(tokens, x.at[0], tok_sem)
    par_copies = [
        pltpu.make_async_copy(a, b, par_sem.at[i])
        for i, (a, b) in enumerate(
            ((taps, taps_v), (residues, res_v), (rates, rates_v), (skip, skip_v))
        )
    ]
    barrier = pltpu.get_barrier_semaphore()

    def greet(c, t):
        pl.semaphore_signal(barrier, inc=1, device_id={"ctx": c, "tp": t}, device_id_type=MESH)

    greet(ctx, partner(1))
    greet(ctx, partner(2))
    greet(ctx, partner(3))

    @pl.when((y == 0) & (xx > 0))
    def _():
        greet(ctx - 1, tp)

    @pl.loop(y + 1, NY)
    def _(k):
        greet(g * NY + k, tp)

    @pl.loop(xx + 1, nx)
    def _(k):
        greet((half * nx + k) * NY + y, tp)

    @pl.when(half == 0)
    def _():
        @pl.loop(xx, nx)
        def _(k):
            greet((nx + k) * NY + y, tp)

    own_copy.start()
    for j in range(3):
        w_copy(0, j).start()
    for c in par_copies:
        c.start()
    for j in range(3):
        w_copy(1, j).start()

    heard = 3 + jnp.where((y == NY - 1) & (xx < nx - 1), 1, 0) + y + xx + half * (xx + 1)
    pl.semaphore_wait(barrier, heard)

    def sib_copy():
        return pltpu.make_async_remote_copy(
            tokens, x.at[1], sib_s, sib_r,
            device_id={"ctx": ctx, "tp": partner(1)}, device_id_type=MESH)

    def piece(i):
        first, column, columns = CHUNKS[i]
        return pl.ds(first, HALF), pl.ds(column, columns)

    def far_copy(i):
        return pltpu.make_async_remote_copy(
            tokens.at[piece(i)], x.at[2, *piece(i)], far_s.at[i], far_r.at[i],
            device_id={"ctx": ctx, "tp": partner(2)}, device_id_type=MESH)

    def fwd_copy(i):
        return pltpu.make_async_remote_copy(
            x.at[2, *piece(i)], x.at[3, *piece(i)], fwd_s.at[i], fwd_r.at[i],
            device_id={"ctx": ctx, "tp": partner(1)}, device_id_type=MESH)

    def cross_copy():
        return pltpu.make_async_remote_copy(
            tokens.at[piece(len(CHUNKS) - 1)], x.at[3, *piece(len(CHUNKS) - 1)], cross_s, cross_r,
            device_id={"ctx": ctx, "tp": partner(3)}, device_id_type=MESH)

    def rim_copy():
        return pltpu.make_async_remote_copy(
            rim_out, rim_in, rim_s, rim_r,
            device_id={"ctx": ctx + 1, "tp": tp}, device_id_type=MESH)

    for i in range(len(CHUNKS)):
        far_copy(i).start()
    cross_copy().start()
    sib_copy().start()

    def answer(sem, c):
        pl.semaphore_signal(sem, inc=1, device_id={"ctx": c, "tp": tp}, device_id_type=MESH)

    @pl.when(y > 0)
    def _():
        answer(rim_ok, ctx - 1)

    @pl.loop(0, y)
    def _(k):
        answer(row_ok, g * NY + k)

    @pl.loop(0, xx)
    def _(k):
        answer(grid_ok, (half * nx + k) * NY + y)

    @pl.when(half == 1)
    def _():
        @pl.loop(0, xx + 1)
        def _(k):
            answer(grid_ok, k * NY + y)

    for c in par_copies:
        c.wait()

    def by_position(ref, first, value):
        count = value.shape[0]
        for c in range(SUBL):
            ref[pl.ds(first + c, count, stride=SUBL), :] = value[:, c * LANE:(c + 1) * LANE]

    for j in range(3):
        by_position(taps_t, j * 3 * SUBL, taps_v[j])
    by_position(res, 0, res_v[...])
    by_position(fac, 0, rates_v[...])
    rate = fac[...]
    for d in range(NY):
        below = (y + NY - d) % NY
        wtot[d] = jnp.exp(-rate * (ROWS * (NY - 1 - below)).astype(F32))
        if d:
            wpre[d - 1] = jnp.exp(-rate * float(ROWS * (d - 1))) * jnp.where(d <= y, 1.0, 0.0)
    fac_step[0] = jnp.exp(-rate * float(ROWS * NY))
    fac_step[1] = jnp.exp(-rate * (ROWS * y).astype(F32))
    fac_part[0] = jnp.exp(-rate * float(ROWS - 2))
    fac_part[1] = jnp.exp(-rate * float(ROWS - HALF - 2))
    fac[...] = jnp.exp(-rate)

    for j in range(3):
        proj[j * M * SUBL:(j * M + PAD) * SUBL, :] = jnp.zeros((PAD * SUBL, LANE), F32)

    def tile_of(q):
        return q // TILES, slice((q % TILES) * TILE, (q % TILES + 1) * TILE)

    own_copy.wait()
    for j in range(3):
        w_copy(0, j).wait()
        w_copy(2, j).start()
        for q in range(j * TILES, (j + 1) * TILES):
            _, cols = tile_of(q)
            acc[q] = jnp.dot(x[0], w[0, j, :, cols], preferred_element_type=F32)
    @pl.when((half == 1) & (xx < nx - 1))
    def _():
        pl.semaphore_wait(grid_ok, nx - 1 - xx)

        @pl.loop(xx + 1, nx)
        def _(k):
            answer(grid_ok, k * NY + y)

    @pl.when(ctx == seam)
    def _():
        answer(seam_ok, seam - NY)

    sib_copy().wait_recv()
    for j in range(3):
        w_copy(1, j).wait()
        w_copy(3, j).start()
        for q in range(j * TILES, (j + 1) * TILES):
            _, cols = tile_of(q)
            acc[q] += jnp.dot(x[1], w[1, j, :, cols], preferred_element_type=F32)

    @pl.when(y < NY - 1)
    def _():
        pl.semaphore_wait(row_ok, NY - 1 - y)

    @pl.when(ctx == seam - NY)
    def _():
        pl.semaphore_wait(seam_ok, 1)
        answer(rim_ok, seam - 1)

    def dots(i, q, slots):
        j, cols = tile_of(q)
        first, column, columns = CHUNKS[i]
        r, k = slice(first, first + HALF), slice(column, column + columns)
        left = jnp.concatenate([x[s, r, k] for s in slots], axis=1)
        right = jnp.concatenate([w[s, j, k, cols] for s in slots], axis=0)
        return jnp.dot(left, right, preferred_element_type=F32)

    def add(i, slots, tiles=range(3 * TILES)):
        r = slice(CHUNKS[i][0], CHUNKS[i][0] + HALF)
        for q in tiles:
            acc[q, r] += dots(i, q, slots)

    def finish(i, q, slots):
        first = CHUNKS[i][0]
        value = acc[q, first:first + HALF] + dots(i, q, slots)
        value = value.astype(BF16).astype(F32)
        start = ((q // TILES) * M + PAD + first) * SUBL + (q % TILES) * (TILE // LANE)
        for c in range(TILE // LANE):
            proj[pl.ds(start + c, HALF, stride=SUBL), :] = value[:, c * LANE:(c + 1) * LANE]

    last = len(CHUNKS) - 1
    for i in range(LATER):
        far_copy(i).wait_recv()
        fwd_copy(i).start()
        if i == 0:
            for j in range(3):
                w_copy(2, j).wait()
        add(i, (2,))
        if i == 0:
            for j in range(3):
                w_copy(3, j).wait()
        fwd_copy(i).wait_recv()
        if i < LATER - 1:
            add(i, (3,))
    for q in range(3 * TILES):
        finish(LATER - 1, q, (3,))

    for j in range(3):
        first = ((j + 1) * M - 2) * SUBL
        rim_out[2 * SUBL * j:2 * SUBL * (j + 1), :] = proj[first:first + 2 * SUBL, :].astype(BF16)

    @pl.when((y < NY - 1) | (ctx == seam - 1))
    def _():
        pl.semaphore_wait(rim_ok, 1)

    @pl.when(ctx < n_ctx - 1)
    def _():
        rim_copy().start()

    def row(j, t):
        first = (j * M + PAD + t) * SUBL
        return proj[pl.ds(pl.multiple_of(first, SUBL), SUBL), :]

    def at(t):
        return pl.ds(pl.multiple_of(t * SUBL, SUBL), SUBL)

    def tap(j, m):
        first = (j * 3 + m) * SUBL
        return taps_t[first:first + SUBL, :]

    shape, flat = (ORDER, SUBL, LANE), (ORDER * SUBL, LANE)

    def mix(j, p0, p1, p2):
        return tap(j, 0) * p0 + tap(j, 1) * p1 + tap(j, 2) * p2

    def own_source(t, keys, values):
        own = (mix(1, *keys) * mix(2, *values)).astype(BF16).astype(F32)
        src[at(t), :] = own
        return own

    zero = jnp.zeros(shape, F32)

    def state_of(start, count, unroll):
        def state_step(i, carry):
            s, k1, k2, v1, v2 = carry
            f = fac[...].reshape(shape)
            for u in range(unroll):
                t = start + i * unroll + u
                k0, v0 = row(1, t), row(2, t)
                s = f * s + own_source(t, (k0, k1, k2), (v0, v1, v2))[None]
                k1, k2, v1, v2 = k0, k1, v0, v1
            return s, k1, k2, v1, v2

        before = [row(j, start - d) for j in (1, 2) for d in (1, 2)]
        return lax.fori_loop(0, count // unroll, state_step, (zero, *before))[0]

    later_state = state_of(HALF + 2, HALF - 2, 9)
    row_tot[0] = later_state.reshape(flat)

    for i in range(LATER, last + 1):
        far_copy(i).wait_recv()
        if i < last:
            fwd_copy(i).start()
        if i > LATER:
            fwd_copy(i - 1).wait_recv()
            add(i - 1, (2, 3), range(0 if i < last else TILES, 3 * TILES))
    cross_copy().wait_recv()
    for q in range(TILES, 3 * TILES):
        finish(last, q, (2, 3))
    early_state = state_of(2, HALF, 8)

    @pl.when(ctx > 0)
    def _():
        rim_copy().wait_recv()
        for j in range(3):
            first = (j * M + PAD - 2) * SUBL
            proj[first:first + 2 * SUBL, :] = rim_in[2 * SUBL * j:2 * SUBL * (j + 1), :].astype(F32)

    rim_state = fac[...].reshape(shape) * own_source(
        0, [row(1, -d) for d in range(3)], [row(2, -d) for d in range(3)])[None]
    rim_state += own_source(
        1, [row(1, 1 - d) for d in range(3)], [row(2, 1 - d) for d in range(3)])[None]
    own_state = row_tot[0] + fac_part[1] * early_state.reshape(flat)
    own_state += fac_part[0] * rim_state.reshape(flat)
    state[...] = own_state.astype(BF16)

    def row_copy(d):
        return pltpu.make_async_remote_copy(
            state, row_in.at[d - 1], row_s.at[d - 1], row_r.at[d - 1],
            device_id={"ctx": ctx - y + (y + d) % NY, "tp": tp}, device_id_type=MESH)

    for d in (2, 1, 3):
        row_copy(d).start()
    row_tot[0] = own_state * wtot[0]

    add(last - 1, (2, 3), range(TILES))
    for q in range(TILES):
        finish(last, q, (2, 3))

    def local_step(i, carry):
        s, g1, g2 = carry
        f, r = fac[...].reshape(shape), res[...].reshape(shape)
        for u in range(8):
            t = i * 8 + u
            own, g0 = src[at(t), :], row(0, t)
            s = f * s + own[None]
            base[at(t), :] = jnp.sum(r * s, axis=0) + skip_v[...] * own
            gate[at(t), :] = tap(0, 0) * g0 + tap(0, 1) * g1 + tap(0, 2) * g2
            g1, g2 = g0, g1
        return s, g1, g2

    lax.fori_loop(0, ROWS // 8, local_step, (zero, row(0, -1), row(0, -2)))

    total = row_tot[0]
    for d in range(1, NY):
        row_copy(d).wait_recv()
        total += wtot[d] * row_in[d - 1].astype(F32)
    row_sum[...] = total.astype(BF16)

    def grid_copy(d):
        return pltpu.make_async_remote_copy(
            row_sum, grid_in.at[d - 1], grid_s.at[d - 1], grid_r.at[d - 1],
            device_id={"ctx": ctx + NY * d, "tp": tp}, device_id_type=MESH)

    @pl.when(half == 0)
    def _():
        pl.semaphore_wait(grid_ok, n_rows - 1 - g)

    for d in range(1, n_rows):
        @pl.when(d < n_rows - g)
        def _(d=d):
            grid_copy(d).start()

    prior = jnp.zeros(flat, F32)
    for d in range(1, NY):
        prior += wpre[d - 1] * row_in[d - 1].astype(F32)
    row_tot[0] = prior

    for d in range(1, NY):
        row_copy(d).wait_send()
    sib_copy().wait_send()
    for i in range(last + 1):
        far_copy(i).wait_send()
        if i < last:
            fwd_copy(i).wait_send()
    cross_copy().wait_send()

    @pl.when(ctx < n_ctx - 1)
    def _():
        rim_copy().wait_send()

    def add_row(k, total):
        d = g - k
        grid_copy(d).wait_recv()
        return fac_step[0] * total + grid_in[d - 1].astype(F32)

    ahead = lax.fori_loop(0, g, add_row, jnp.zeros(flat, F32))
    ahead = row_tot[0] + fac_step[1] * ahead

    def last_rows(first, u):
        f = fac[...].reshape(shape)
        for b in range(STEP):
            t = first + b
            u = u * f
            done[at(t), :] = gate[at(t), :] * (jnp.sum(u, axis=0) + base[at(t), :])
        return u

    def emit(a):
        rows = pl.ds(pl.multiple_of(a * STEP, STEP), STEP)
        for c in range(SUBL):
            value = done[pl.ds(a * STEP * SUBL + c, STEP, stride=SUBL), :]
            out[rows, c * LANE:(c + 1) * LANE] = value.astype(BF16)

    def last_step(a, u):
        emit(a - 1)
        return last_rows(a * STEP, u)

    weighted = last_rows(0, (res[...] * ahead).reshape(shape))
    lax.fori_loop(1, ROWS // STEP, last_step, weighted)
    emit(ROWS // STEP - 1)

    @pl.loop(1, n_rows - g)
    def _(d):
        grid_copy(d).wait_send()


def shards(tokens, proj_weight, short_taps, residues, rates, skip):
    hbm = pl.BlockSpec(memory_space=pltpu.HBM)
    n_rows = lax.axis_size("ctx") // NY
    chunks = len(CHUNKS)
    flat = (ORDER * SUBL, LANE)
    dma = pltpu.SemaphoreType.DMA
    return pl.pallas_call(
        kernel,
        out_shape=pltpu.VMEM((ROWS, WIDTH), BF16),
        in_specs=[hbm] * 6,
        out_specs=pl.BlockSpec(memory_space=pltpu.VMEM),
        scratch_shapes=[
            pltpu.VMEM((4, 3, WIDTH, WIDTH), BF16),
            pltpu.VMEM((4, ROWS, WIDTH), BF16),
            pltpu.VMEM((3 * TILES, ROWS, TILE), F32),
            pltpu.VMEM((3 * M * SUBL, LANE), F32),
            pltpu.VMEM((ROWS * SUBL, LANE), F32),
            pltpu.VMEM((ROWS * SUBL, LANE), F32),
            pltpu.VMEM((ROWS * SUBL, LANE), F32),
            pltpu.VMEM((ROWS * SUBL, LANE), F32),
            pltpu.VMEM(flat, F32),
            pltpu.VMEM((2, *flat), F32),
            pltpu.VMEM((2, *flat), F32),
            pltpu.VMEM(flat, F32),
            pltpu.VMEM((3 * 2 * SUBL, LANE), BF16),
            pltpu.VMEM((3 * 2 * SUBL, LANE), BF16),
            pltpu.VMEM((3, 3, WIDTH), F32),
            pltpu.VMEM((9 * SUBL, LANE), F32),
            pltpu.VMEM((ORDER, WIDTH), F32),
            pltpu.VMEM((ORDER, WIDTH), F32),
            pltpu.VMEM((SUBL, LANE), F32),
            pltpu.VMEM(flat, BF16),
            pltpu.VMEM(flat, BF16),
            pltpu.VMEM((NY - 1, *flat), BF16),
            pltpu.VMEM((1, *flat), F32),
            pltpu.VMEM((n_rows - 1, *flat), BF16),
            pltpu.VMEM((NY - 1, *flat), F32),
            pltpu.VMEM((NY, *flat), F32),
            dma((4, 3)),
            dma,
            dma((4,)),
            dma, dma,
            dma((chunks,)), dma((chunks,)),
            dma((chunks - 1,)), dma((chunks - 1,)),
            dma, dma,
            dma, dma,
            dma((NY - 1,)), dma((NY - 1,)),
            dma((n_rows - 1,)), dma((n_rows - 1,)),
            *[pltpu.SemaphoreType.REGULAR] * 4,
        ],
        compiler_params=pltpu.CompilerParams(
            collective_id=0, has_side_effects=True, vmem_limit_bytes=56 * 2**20),
        name="hyena",
    )(tokens, proj_weight, short_taps, residues.T, rates.T, skip.reshape(SUBL, LANE))


def solution(mesh):
    return jax.shard_map(
        shards,
        mesh=mesh,
        in_specs=(
            P("ctx", "tp"),
            P(None, None, "tp"),
            P(None, None, "tp"),
            P("tp", None),
            P("tp", None),
            P("tp"),
        ),
        out_specs=P("ctx", "tp"),
        check_vma=False,
    )
```

```python
import jax
import jax.numpy as jnp
from jax import lax
from jax.experimental import pallas as pl
from jax.experimental.pallas import tpu as pltpu
from jax.sharding import PartitionSpec as P

MESH = pl.DeviceIdType.MESH
F32, BF16 = jnp.float32, jnp.bfloat16

ROWS = 256
HALF = 128
PAD = 8
M = PAD + ROWS
WIDTH = 1024
ORDER = 16
LANE, SUBL = 128, 8
TILE = 256
TILES = WIDTH // TILE
NY = 4
STEP = 16
CHUNKS = (
    (HALF, 0, 512), (HALF, 512, 512),
    (0, 0, 512), (0, 512, 256), (0, 768, 128), (0, 896, 128),
)
LATER = 2


def kernel(
    tokens, weight, taps, residues, rates, skip, out,
    w, x, acc, proj, src, base, gate, done, fac, fac_step, fac_part, res, spread, rim_out, rim_in,
    taps_v, taps_t, rates_v, res_v, skip_v, state, row_sum, row_in, row_tot, grid_in, wpre, wtot,
    w_sem, tok_sem, par_sem, sib_s, sib_r, far_s, far_r, fwd_s, fwd_r, cross_s, cross_r,
    rim_s, rim_r, row_s, row_r, grid_s, grid_r, rim_ok, row_ok, grid_ok, seam_ok,
):
    ctx, tp = lax.axis_index("ctx"), lax.axis_index("tp")
    n_ctx = lax.axis_size("ctx")
    n_rows = n_ctx // NY
    y, g = ctx % NY, ctx // NY
    nx = n_rows // 2
    half, xx = g // nx, g % nx
    seam = nx * NY

    def partner(s):
        return (tp + 1 - 2 * (tp % 2), (tp + 2) % 4, 3 - tp)[s - 1] if s else tp

    def w_copy(s, j):
        rows = pl.ds(pl.multiple_of(partner(s) * WIDTH, WIDTH), WIDTH)
        return pltpu.make_async_copy(weight.at[j, rows, :], w.at[s, j], w_sem.at[s, j])

    own_copy = pltpu.make_async_copy(tokens, x.at[0], tok_sem)
    par_copies = [
        pltpu.make_async_copy(a, b, par_sem.at[i])
        for i, (a, b) in enumerate(
            ((taps, taps_v), (residues, res_v), (rates, rates_v), (skip, skip_v))
        )
    ]
    barrier = pltpu.get_barrier_semaphore()

    def greet(c, t):
        pl.semaphore_signal(barrier, inc=1, device_id={"ctx": c, "tp": t}, device_id_type=MESH)

    greet(ctx, partner(1))
    greet(ctx, partner(2))
    greet(ctx, partner(3))

    @pl.when((y == 0) & (xx > 0))
    def _():
        greet(ctx - 1, tp)

    @pl.loop(y + 1, NY)
    def _(k):
        greet(g * NY + k, tp)

    @pl.loop(xx + 1, nx)
    def _(k):
        greet((half * nx + k) * NY + y, tp)

    @pl.when(half == 0)
    def _():
        @pl.loop(xx, nx)
        def _(k):
            greet((nx + k) * NY + y, tp)

    own_copy.start()
    for j in range(3):
        w_copy(0, j).start()
    for c in par_copies:
        c.start()
    for j in range(3):
        w_copy(1, j).start()

    heard = 3 + jnp.where((y == NY - 1) & (xx < nx - 1), 1, 0) + y + xx + half * (xx + 1)
    pl.semaphore_wait(barrier, heard)

    def sib_copy():
        return pltpu.make_async_remote_copy(
            tokens, x.at[1], sib_s, sib_r,
            device_id={"ctx": ctx, "tp": partner(1)}, device_id_type=MESH)

    def piece(i):
        first, column, columns = CHUNKS[i]
        return pl.ds(first, HALF), pl.ds(column, columns)

    def far_copy(i):
        return pltpu.make_async_remote_copy(
            tokens.at[piece(i)], x.at[2, *piece(i)], far_s.at[i], far_r.at[i],
            device_id={"ctx": ctx, "tp": partner(2)}, device_id_type=MESH)

    def fwd_copy(i):
        return pltpu.make_async_remote_copy(
            x.at[2, *piece(i)], x.at[3, *piece(i)], fwd_s.at[i], fwd_r.at[i],
            device_id={"ctx": ctx, "tp": partner(1)}, device_id_type=MESH)

    def cross_copy():
        return pltpu.make_async_remote_copy(
            tokens.at[piece(len(CHUNKS) - 1)], x.at[3, *piece(len(CHUNKS) - 1)], cross_s, cross_r,
            device_id={"ctx": ctx, "tp": partner(3)}, device_id_type=MESH)

    def rim_copy():
        return pltpu.make_async_remote_copy(
            rim_out, rim_in, rim_s, rim_r,
            device_id={"ctx": ctx + 1, "tp": tp}, device_id_type=MESH)

    for i in range(len(CHUNKS)):
        far_copy(i).start()
    cross_copy().start()
    sib_copy().start()

    def answer(sem, c):
        pl.semaphore_signal(sem, inc=1, device_id={"ctx": c, "tp": tp}, device_id_type=MESH)

    @pl.when(y > 0)
    def _():
        answer(rim_ok, ctx - 1)

    @pl.loop(0, y)
    def _(k):
        answer(row_ok, g * NY + k)

    @pl.loop(0, xx)
    def _(k):
        answer(grid_ok, (half * nx + k) * NY + y)

    @pl.when(half == 1)
    def _():
        @pl.loop(0, xx + 1)
        def _(k):
            answer(grid_ok, k * NY + y)

    for c in par_copies:
        c.wait()

    def by_position(ref, first, value):
        count = value.shape[0]
        for c in range(SUBL):
            ref[pl.ds(first + c, count, stride=SUBL), :] = value[:, c * LANE:(c + 1) * LANE]

    for j in range(3):
        by_position(taps_t, j * 3 * SUBL, taps_v[j])
    by_position(spread, 0, res_v[...])
    res[...] = spread[0:ORDER * SUBL, :]
    by_position(spread, 0, rates_v[...])
    rate = spread[0:ORDER * SUBL, :]
    for d in range(NY):
        below = (y + NY - d) % NY
        wtot[d] = jnp.exp(-rate * (ROWS * (NY - 1 - below)).astype(F32))
        if d:
            wpre[d - 1] = jnp.exp(-rate * float(ROWS * (d - 1))) * jnp.where(d <= y, 1.0, 0.0)
    fac_step[0] = jnp.exp(-rate * float(ROWS * NY))
    fac_step[1] = jnp.exp(-rate * (ROWS * y).astype(F32))
    fac_part[0] = jnp.exp(-rate * float(ROWS - 2))
    fac_part[1] = jnp.exp(-rate * float(ROWS - HALF - 2))
    fac[...] = jnp.exp(-rate)

    for j in range(3):
        proj[j * M * SUBL:(j * M + PAD) * SUBL, :] = jnp.zeros((PAD * SUBL, LANE), F32)

    def tile_of(q):
        return q // TILES, slice((q % TILES) * TILE, (q % TILES + 1) * TILE)

    own_copy.wait()
    for j in range(3):
        w_copy(0, j).wait()
        w_copy(2, j).start()
        for q in range(j * TILES, (j + 1) * TILES):
            _, cols = tile_of(q)
            acc[q] = jnp.dot(x[0], w[0, j, :, cols], preferred_element_type=F32)
    @pl.when((half == 1) & (xx < nx - 1))
    def _():
        pl.semaphore_wait(grid_ok, nx - 1 - xx)

        @pl.loop(xx + 1, nx)
        def _(k):
            answer(grid_ok, k * NY + y)

    @pl.when(ctx == seam)
    def _():
        answer(seam_ok, seam - NY)

    sib_copy().wait_recv()
    for j in range(3):
        w_copy(1, j).wait()
        w_copy(3, j).start()
        for q in range(j * TILES, (j + 1) * TILES):
            _, cols = tile_of(q)
            acc[q] += jnp.dot(x[1], w[1, j, :, cols], preferred_element_type=F32)

    @pl.when(y < NY - 1)
    def _():
        pl.semaphore_wait(row_ok, NY - 1 - y)

    @pl.when(ctx == seam - NY)
    def _():
        pl.semaphore_wait(seam_ok, 1)
        answer(rim_ok, seam - 1)

    def dots(i, q, slots):
        j, cols = tile_of(q)
        first, column, columns = CHUNKS[i]
        r, k = slice(first, first + HALF), slice(column, column + columns)
        left = jnp.concatenate([x[s, r, k] for s in slots], axis=1)
        right = jnp.concatenate([w[s, j, k, cols] for s in slots], axis=0)
        return jnp.dot(left, right, preferred_element_type=F32)

    def add(i, slots, tiles=range(3 * TILES)):
        r = slice(CHUNKS[i][0], CHUNKS[i][0] + HALF)
        for q in tiles:
            acc[q, r] += dots(i, q, slots)

    def finish(i, q, slots):
        first = CHUNKS[i][0]
        value = acc[q, first:first + HALF] + dots(i, q, slots)
        value = value.astype(BF16).astype(F32)
        start = ((q // TILES) * M + PAD + first) * SUBL + (q % TILES) * (TILE // LANE)
        for c in range(TILE // LANE):
            proj[pl.ds(start + c, HALF, stride=SUBL), :] = value[:, c * LANE:(c + 1) * LANE]

    last = len(CHUNKS) - 1
    for i in range(LATER):
        far_copy(i).wait_recv()
        fwd_copy(i).start()
        if i == 0:
            for j in range(3):
                w_copy(2, j).wait()
        add(i, (2,))
        if i == 0:
            for j in range(3):
                w_copy(3, j).wait()
        fwd_copy(i).wait_recv()
        if i < LATER - 1:
            add(i, (3,))
    for q in range(3 * TILES):
        finish(LATER - 1, q, (3,))

    for j in range(3):
        first = ((j + 1) * M - 2) * SUBL
        rim_out[2 * SUBL * j:2 * SUBL * (j + 1), :] = proj[first:first + 2 * SUBL, :].astype(BF16)

    @pl.when((y < NY - 1) | (ctx == seam - 1))
    def _():
        pl.semaphore_wait(rim_ok, 1)

    @pl.when(ctx < n_ctx - 1)
    def _():
        rim_copy().start()

    def row(j, t):
        first = (j * M + PAD + t) * SUBL
        return proj[pl.ds(pl.multiple_of(first, SUBL), SUBL), :]

    def at(t):
        return pl.ds(pl.multiple_of(t * SUBL, SUBL), SUBL)

    def tap(j, m):
        first = (j * 3 + m) * SUBL
        return taps_t[first:first + SUBL, :]

    shape, flat = (ORDER, SUBL, LANE), (ORDER * SUBL, LANE)

    def mix(j, p0, p1, p2):
        return tap(j, 0) * p0 + tap(j, 1) * p1 + tap(j, 2) * p2

    def own_source(t, keys, values):
        own = (mix(1, *keys) * mix(2, *values)).astype(BF16).astype(F32)
        src[at(t), :] = own
        return own

    zero = jnp.zeros(shape, F32)

    def state_of(start, count, unroll):
        def state_step(i, carry):
            s, k1, k2, v1, v2 = carry
            f = fac[...].reshape(shape)
            for u in range(unroll):
                t = start + i * unroll + u
                k0, v0 = row(1, t), row(2, t)
                s = f * s + own_source(t, (k0, k1, k2), (v0, v1, v2))[None]
                k1, k2, v1, v2 = k0, k1, v0, v1
            return s, k1, k2, v1, v2

        before = [row(j, start - d) for j in (1, 2) for d in (1, 2)]
        return lax.fori_loop(0, count // unroll, state_step, (zero, *before))[0]

    later_state = state_of(HALF + 2, HALF - 2, 9)
    row_tot[0] = later_state.reshape(flat)

    for i in range(LATER, last + 1):
        far_copy(i).wait_recv()
        if i < last:
            fwd_copy(i).start()
        if i > LATER:
            fwd_copy(i - 1).wait_recv()
            add(i - 1, (2, 3), range(0 if i < last else TILES, 3 * TILES))
    cross_copy().wait_recv()
    for q in range(TILES, 3 * TILES):
        finish(last, q, (2, 3))
    early_state = state_of(2, HALF, 8)

    @pl.when(ctx > 0)
    def _():
        rim_copy().wait_recv()
        for j in range(3):
            first = (j * M + PAD - 2) * SUBL
            proj[first:first + 2 * SUBL, :] = rim_in[2 * SUBL * j:2 * SUBL * (j + 1), :].astype(F32)

    rim_state = fac[...].reshape(shape) * own_source(
        0, [row(1, -d) for d in range(3)], [row(2, -d) for d in range(3)])[None]
    rim_state += own_source(
        1, [row(1, 1 - d) for d in range(3)], [row(2, 1 - d) for d in range(3)])[None]
    own_state = row_tot[0] + fac_part[1] * early_state.reshape(flat)
    own_state += fac_part[0] * rim_state.reshape(flat)
    state[...] = own_state.astype(BF16)

    def row_copy(d):
        return pltpu.make_async_remote_copy(
            state, row_in.at[d - 1], row_s.at[d - 1], row_r.at[d - 1],
            device_id={"ctx": ctx - y + (y + d) % NY, "tp": tp}, device_id_type=MESH)

    for d in (2, 1, 3):
        row_copy(d).start()
    row_tot[0] = own_state * wtot[0]

    add(last - 1, (2, 3), range(TILES))
    for q in range(TILES):
        finish(last, q, (2, 3))

    def local_step(i, carry):
        s, g1, g2 = carry
        f, r = fac[...].reshape(shape), res[...].reshape(shape)
        for u in range(8):
            t = i * 8 + u
            own, g0 = src[at(t), :], row(0, t)
            s = f * s + own[None]
            base[at(t), :] = jnp.sum(r * s, axis=0) + skip_v[...] * own
            gate[at(t), :] = tap(0, 0) * g0 + tap(0, 1) * g1 + tap(0, 2) * g2
            g1, g2 = g0, g1
        return s, g1, g2

    lax.fori_loop(0, ROWS // 8, local_step, (zero, row(0, -1), row(0, -2)))

    total = row_tot[0]
    for d in range(1, NY):
        row_copy(d).wait_recv()
        total += wtot[d] * row_in[d - 1].astype(F32)
    row_sum[...] = total.astype(BF16)

    def grid_copy(d):
        return pltpu.make_async_remote_copy(
            row_sum, grid_in.at[d - 1], grid_s.at[d - 1], grid_r.at[d - 1],
            device_id={"ctx": ctx + NY * d, "tp": tp}, device_id_type=MESH)

    @pl.when(half == 0)
    def _():
        pl.semaphore_wait(grid_ok, n_rows - 1 - g)

    for d in range(1, n_rows):
        @pl.when(d < n_rows - g)
        def _(d=d):
            grid_copy(d).start()

    prior = jnp.zeros(flat, F32)
    for d in range(1, NY):
        prior += wpre[d - 1] * row_in[d - 1].astype(F32)
    row_tot[0] = prior

    for d in range(1, NY):
        row_copy(d).wait_send()
    sib_copy().wait_send()
    for i in range(last + 1):
        far_copy(i).wait_send()
        if i < last:
            fwd_copy(i).wait_send()
    cross_copy().wait_send()

    @pl.when(ctx < n_ctx - 1)
    def _():
        rim_copy().wait_send()

    def add_row(k, total):
        d = g - k
        grid_copy(d).wait_recv()
        return fac_step[0] * total + grid_in[d - 1].astype(F32)

    ahead = lax.fori_loop(0, g, add_row, jnp.zeros(flat, F32))
    ahead = row_tot[0] + fac_step[1] * ahead

    def last_rows(first, u):
        f = fac[...].reshape(shape)
        for b in range(STEP):
            t = first + b
            u = u * f
            done[at(t), :] = gate[at(t), :] * (jnp.sum(u, axis=0) + base[at(t), :])
        return u

    def emit(a):
        rows = pl.ds(pl.multiple_of(a * STEP, STEP), STEP)
        for c in range(SUBL):
            value = done[pl.ds(a * STEP * SUBL + c, STEP, stride=SUBL), :]
            out[rows, c * LANE:(c + 1) * LANE] = value.astype(BF16)

    def last_step(a, u):
        emit(a - 1)
        return last_rows(a * STEP, u)

    weighted = last_rows(0, (res[...] * ahead).reshape(shape))
    lax.fori_loop(1, ROWS // STEP, last_step, weighted)
    emit(ROWS // STEP - 1)

    @pl.loop(1, n_rows - g)
    def _(d):
        grid_copy(d).wait_send()


def shards(tokens, proj_weight, short_taps, residues, rates, skip):
    hbm = pl.BlockSpec(memory_space=pltpu.HBM)
    n_rows = lax.axis_size("ctx") // NY
    chunks = len(CHUNKS)
    flat = (ORDER * SUBL, LANE)
    dma = pltpu.SemaphoreType.DMA
    return pl.pallas_call(
        kernel,
        out_shape=pltpu.VMEM((ROWS, WIDTH), BF16),
        in_specs=[hbm] * 6,
        out_specs=pl.BlockSpec(memory_space=pltpu.VMEM),
        scratch_shapes=[
            pltpu.VMEM((4, 3, WIDTH, WIDTH), BF16),
            pltpu.VMEM((4, ROWS, WIDTH), BF16),
            pltpu.VMEM((3 * TILES, ROWS, TILE), F32),
            pltpu.VMEM(((3 * M + 1) * SUBL, LANE), F32),
            pltpu.VMEM((ROWS * SUBL, LANE), F32),
            pltpu.VMEM((ROWS * SUBL, LANE), F32),
            pltpu.VMEM((ROWS * SUBL, LANE), F32),
            pltpu.VMEM(((ROWS + 1) * SUBL, LANE), F32),
            pltpu.VMEM(flat, F32),
            pltpu.VMEM((2, *flat), F32),
            pltpu.VMEM((2, *flat), F32),
            pltpu.VMEM(flat, F32),
            pltpu.VMEM(((ORDER + 1) * SUBL, LANE), F32),
            pltpu.VMEM((3 * 2 * SUBL, LANE), BF16),
            pltpu.VMEM((3 * 2 * SUBL, LANE), BF16),
            pltpu.VMEM((3, 3, WIDTH), F32),
            pltpu.VMEM((10 * SUBL, LANE), F32),
            pltpu.VMEM((ORDER, WIDTH), F32),
            pltpu.VMEM((ORDER, WIDTH), F32),
            pltpu.VMEM((SUBL, LANE), F32),
            pltpu.VMEM(flat, BF16),
            pltpu.VMEM(flat, BF16),
            pltpu.VMEM((NY - 1, *flat), BF16),
            pltpu.VMEM((1, *flat), F32),
            pltpu.VMEM((n_rows - 1, *flat), BF16),
            pltpu.VMEM((NY - 1, *flat), F32),
            pltpu.VMEM((NY, *flat), F32),
            dma((4, 3)),
            dma,
            dma((4,)),
            dma, dma,
            dma((chunks,)), dma((chunks,)),
            dma((chunks - 1,)), dma((chunks - 1,)),
            dma, dma,
            dma, dma,
            dma((NY - 1,)), dma((NY - 1,)),
            dma((n_rows - 1,)), dma((n_rows - 1,)),
            *[pltpu.SemaphoreType.REGULAR] * 4,
        ],
        compiler_params=pltpu.CompilerParams(
            collective_id=0, has_side_effects=True, vmem_limit_bytes=56 * 2**20),
        name="hyena",
    )(tokens, proj_weight, short_taps, residues.T, rates.T, skip.reshape(SUBL, LANE))


def solution(mesh):
    return jax.shard_map(
        shards,
        mesh=mesh,
        in_specs=(
            P("ctx", "tp"),
            P(None, None, "tp"),
            P(None, None, "tp"),
            P("tp", None),
            P("tp", None),
            P("tp"),
        ),
        out_specs=P("ctx", "tp"),
        check_vma=False,
    )
```
